32 devices in a mesh: gx: 16 (over z, y, x), sa: 2 (over core).
Axes of the slice: x: 2, y: 2, z: 4, core: 2. Of those that a mesh axis runs over, the one named last changes fastest.
Arguments:
- inputs: bfloat16 [2, 16, 64, 128, 128], P('sa', None, 'gx'), may hold values from -6 to 6
- preact: bfloat16 [2, 16, 64, 128, 128], P('sa', None, 'gx'), may hold values from -6 to 6
- cotangent: bfloat16 [2, 16, 64, 128, 128], P('sa', None, 'gx'), may hold values from -6 to 6
- mode_weight: bfloat16 [16, 16, 2048, 128], P(None, None, 'gx'), may hold values from -1 to 1
- bypass_weight: bfloat16 [16, 16], replicated, may hold values from -1.5 to 1.5
Outputs:
- input_grad: bfloat16 [2, 16, 64, 128, 128], P('sa', None, 'gx')
- mode_grad: float32 [16, 16, 2048, 128], P(None, None, ('gx', 'sa'))
The draws below stay inside these ranges and needn't reach their ends.
All inputs are finite; a program needn't handle non-finite values.
Results may differ from the reference program's by a relative error of at most 0.0097.
Values may be sent and summed in bfloat16 or wider, within the bound.
A program may use at most 128 MiB of HBM per device.

```python
import math
import jax
import jax.numpy as jnp
from jax import lax

C = 16
SY = 128
ST = 128
MX = 64
MY = 64
MT = 32
X = 64
PAIRS = 2048
NS = 2


def block_levels(stream_key, extent, shards, least, high):
    def one(dim, blocks):
        draws = jax.random.uniform(jax.random.fold_in(jax.random.fold_in(stream_key, 6), dim), (blocks,), jnp.float32, least / len(shards), high / len(shards))
        return jnp.repeat(jnp.exp(draws), extent[dim] // blocks).reshape((-1,) + (1,) * (len(extent) - dim - 1))

    gain = one(*shards[0])
    for cut in shards[1:]:
        gain = gain * one(*cut)
    return gain


def noise(own_key, extent, scale, reach, shards=(), kind=jnp.bfloat16):
    loudness = block_levels(own_key, extent, shards, -0.22, 0.18) if shards else 1.0
    array = jax.random.normal(own_key, extent, jnp.float32) * scale * loudness
    return jnp.minimum(jnp.maximum(array, -reach), reach).astype(kind)


def setup_inputs(seed: int = 0) -> dict:
    splits = jax.random.split(jax.random.key(seed), 6)
    inputs = noise(splits[0], (NS, C, X, SY, ST), 1.0, 6.0, ((0, 2), (2, 16)))
    preact = noise(splits[1], (NS, C, X, SY, ST), 1.5, 6.0, ((0, 2), (2, 16)))
    cotangent = noise(splits[2], (NS, C, X, SY, ST), 1.0, 6.0, ((0, 2), (2, 16)))
    mode_weight = noise(splits[3], (C, C, PAIRS, 2 * MX), (2 * C) ** -0.5, 1.0, ((2, 16),))
    bypass_weight = noise(splits[4], (C, C), C ** -0.5, 1.5)
    return {"inputs": inputs, "preact": preact, "cotangent": cotangent, "mode_weight": mode_weight, "bypass_weight": bypass_weight}


root_half = math.sqrt(0.5)
gauss_norm = 1.0 / math.sqrt(2.0 * math.pi)

def tables(kept_count, length, two_sided):
    frequency = jnp.arange(kept_count, dtype=jnp.int32)
    if two_sided:
        frequency = jnp.where(frequency < kept_count // 2, frequency, frequency + (length - kept_count))
    position = jnp.arange(length, dtype=jnp.int32)
    product = frequency[:, None] * position[None, :] % length
    phase_angle = product.astype(jnp.float32) * (2.0 * math.pi / length)
    return (jnp.cos(phase_angle).astype(jnp.bfloat16), jnp.sin(phase_angle).astype(jnp.bfloat16))

def gelu_backward(pieces):
    values = pieces[0].astype(jnp.float32)
    slope = 0.5 * (1.0 + jax.scipy.special.erf(values * root_half)) + values * jnp.exp(-0.5 * values * values) * gauss_norm
    return (pieces[1].astype(jnp.float32) * slope).astype(jnp.bfloat16)

def gradient_term(input_hat, grad_hat, half):
    input_real = input_hat[..., :half].astype(jnp.float32)[:, None]
    input_imag = input_hat[..., half:].astype(jnp.float32)[:, None]
    grad_real = grad_hat[..., :half].astype(jnp.float32)[None]
    grad_imag = grad_hat[..., half:].astype(jnp.float32)[None]
    return jnp.concatenate([input_real * grad_real + input_imag * grad_imag, input_real * grad_imag - input_imag * grad_real], axis=-1)

def reference(inputs, preact, cotangent, mode_weight, bypass_weight):
    pair_count = MY * MT
    cell_count = X * SY * ST
    scale_in = float(MX * pair_count * cell_count) ** (-0.25)
    scale_out = float(cell_count) ** (-0.5)
    cosine_time, sine_time = tables(MT, ST, False)
    cosine_y, sine_y = tables(MY, SY, True)
    cosine_x, sine_x = tables(MX, X, True)
    forward_time = jnp.concatenate([cosine_time.T, -sine_time.T], axis=1)
    inverse_time = jnp.concatenate([cosine_time, -sine_time], axis=0)
    plane_table = jnp.stack([jnp.stack([cosine_y, sine_y], -1), jnp.stack([-sine_y, cosine_y], -1)]).astype(jnp.float32)
    x_forward = jnp.stack([jnp.concatenate([cosine_x, -sine_x], 0).T, jnp.concatenate([sine_x, cosine_x], 0).T], 1).astype(jnp.float32)
    x_inverse = jnp.stack([jnp.concatenate([cosine_x, -sine_x], 0), jnp.concatenate([sine_x, cosine_x], 0)], -1).astype(jnp.float32)

    def forward_field(field):
        sectioned = jnp.dot(field.reshape(-1, ST), forward_time, preferred_element_type=jnp.float32).astype(jnp.bfloat16)
        sectioned = sectioned.reshape(X, SY, 2, MT).astype(jnp.float32)
        plane = jnp.einsum('xyqk,ajyq->xajk', sectioned, plane_table).astype(jnp.bfloat16)
        plane = plane.reshape(X, 2, pair_count).astype(jnp.float32)
        return jnp.einsum('xqp,xqr->pr', plane, x_forward)

    def scaled_input(field):
        return (scale_in * forward_field(field)).astype(jnp.bfloat16)

    def scaled_grad(field):
        return (scale_out * forward_field(field)).astype(jnp.bfloat16)
    grad_total = jnp.zeros((C, C, pair_count, 2 * MX), jnp.float32)
    results = []
    for sample in range(NS):
        dz_field = lax.map(gelu_backward, (preact[sample], cotangent[sample]))
        input_hat = lax.map(scaled_input, inputs[sample])
        grad_hat = lax.map(scaled_grad, dz_field)
        grad_total = grad_total + gradient_term(input_hat, grad_hat, MX)
        grad_real = grad_hat[..., :MX].astype(jnp.float32)
        grad_imag = grad_hat[..., MX:].astype(jnp.float32)

        def adjoint_row(weight_row):
            weights = weight_row.astype(jnp.float32)
            real_part = lax.optimization_barrier(jnp.sum(weights[..., :MX] * grad_real + weights[..., MX:] * grad_imag, axis=0))
            imag_part = lax.optimization_barrier(jnp.sum(weights[..., :MX] * grad_imag - weights[..., MX:] * grad_real, axis=0))
            return jnp.concatenate([real_part, imag_part], axis=-1).astype(jnp.bfloat16)
        back_hat = lax.map(adjoint_row, mode_weight)

        def inverse_field(pieces):
            back_block, bypass_row = pieces
            grid_rows = jnp.einsum('pr,rxq->xqp', back_block.astype(jnp.float32), x_inverse).astype(jnp.bfloat16)
            grid_rows = grid_rows.reshape(X, 2, MY, MT).astype(jnp.float32)
            joined = jnp.einsum('xajk,ajyq->xyqk', grid_rows, plane_table).astype(jnp.bfloat16)
            spectral = jnp.dot(joined.reshape(-1, 2 * MT), inverse_time, preferred_element_type=jnp.float32)
            spectral = spectral.reshape(X, SY, ST)
            bypass = jnp.dot(bypass_row[None, :], dz_field.reshape(C, -1), preferred_element_type=jnp.float32).reshape(X, SY, ST)
            return (scale_in * spectral + bypass).astype(jnp.bfloat16)
        results.append(lax.map(inverse_field, (back_hat, bypass_weight)))
    return (jnp.stack(results), grad_total)
```

```python
import functools
import math

import jax
import jax.numpy as jnp
import numpy as np
from jax import lax
from jax.experimental import pallas as pl
from jax.experimental.pallas import tpu as pltpu
from jax.sharding import PartitionSpec as P

MY = 64
MT = 32


root_half = math.sqrt(0.5)
gauss_norm = 1.0 / math.sqrt(2.0 * math.pi)


def tables(kept_count, length, two_sided):
    frequency = jnp.arange(kept_count, dtype=jnp.int32)
    if two_sided:
        frequency = jnp.where(
            frequency < kept_count // 2, frequency, frequency + (length - kept_count)
        )
    position = jnp.arange(length, dtype=jnp.int32)
    product = frequency[:, None] * position[None, :] % length
    phase_angle = product.astype(jnp.float32) * (2.0 * math.pi / length)
    return (jnp.cos(phase_angle).astype(jnp.bfloat16), jnp.sin(phase_angle).astype(jnp.bfloat16))


def gelu_backward(preact_block, cotangent_block):
    values = preact_block.astype(jnp.float32)
    slope = (
        0.5 * (1.0 + jax.scipy.special.erf(values * root_half))
        + values * jnp.exp(-0.5 * values * values) * gauss_norm
    )
    return (cotangent_block.astype(jnp.float32) * slope).astype(jnp.bfloat16)


def gradient_term(input_hat, grad_hat, half):
    input_real = input_hat[..., :half].astype(jnp.float32)[:, None]
    input_imag = input_hat[..., half:].astype(jnp.float32)[:, None]
    grad_real = grad_hat[..., :half].astype(jnp.float32)[None]
    grad_imag = grad_hat[..., half:].astype(jnp.float32)[None]
    return jnp.concatenate(
        [
            input_real * grad_real + input_imag * grad_imag,
            input_real * grad_imag - input_imag * grad_real,
        ],
        axis=-1,
    )


def plain_shards(inputs, preact, cotangent, mode_weight, bypass_weight):
    channels = inputs.shape[1]
    slab_cells = inputs.shape[2]
    cells_y = inputs.shape[3]
    cells_time = inputs.shape[4]
    devices_x = lax.axis_size("gx")
    cells_x = slab_cells * devices_x
    modes_x = mode_weight.shape[3] // 2
    modes_y = MY
    modes_time = MT
    pair_count = modes_y * modes_time
    cell_count = cells_x * cells_y * cells_time
    scale_in = float(modes_x * pair_count * cell_count) ** (-0.25)
    scale_out = float(cell_count) ** (-0.5)
    cosine_time, sine_time = tables(modes_time, cells_time, False)
    cosine_y, sine_y = tables(modes_y, cells_y, True)
    cosine_x, sine_x = tables(modes_x, cells_x, True)
    forward_time = jnp.concatenate([cosine_time.T, -sine_time.T], axis=1)
    inverse_time = jnp.concatenate([cosine_time, -sine_time], axis=0)
    plane_table = jnp.stack([jnp.stack([cosine_y, sine_y], -1), jnp.stack([-sine_y, cosine_y], -1)])
    x_forward = jnp.stack(
        [jnp.concatenate([cosine_x, -sine_x], 0).T, jnp.concatenate([sine_x, cosine_x], 0).T], 1
    )
    x_inverse = jnp.stack(
        [jnp.concatenate([cosine_x, -sine_x], 0), jnp.concatenate([sine_x, cosine_x], 0)], -1
    )

    def spectra(field):
        sectioned = jnp.dot(
            field.reshape(-1, cells_time), forward_time, preferred_element_type=jnp.float32
        ).astype(jnp.bfloat16)
        sectioned = sectioned.reshape(channels, slab_cells, cells_y, 2, modes_time)
        plane = jnp.einsum(
            "cxyqk,ajyq->jkcxa", sectioned, plane_table, preferred_element_type=jnp.float32
        ).astype(jnp.bfloat16)
        return plane.reshape(pair_count, channels, slab_cells, 2)

    def x_transform(block, factor):
        summed = jnp.einsum("pcxq,xqr->cpr", block, x_forward, preferred_element_type=jnp.float32)
        return (factor * summed).astype(jnp.bfloat16)

    dz_field = gelu_backward(preact[0], cotangent[0])
    input_hat = x_transform(
        lax.all_to_all(spectra(inputs[0]), "gx", split_axis=0, concat_axis=2, tiled=True), scale_in
    )
    grad_hat = x_transform(
        lax.all_to_all(spectra(dz_field), "gx", split_axis=0, concat_axis=2, tiled=True), scale_out
    )
    mode_grad = lax.psum_scatter(
        gradient_term(input_hat, grad_hat, modes_x).astype(jnp.bfloat16),
        "sa",
        scatter_dimension=2,
        tiled=True,
    ).astype(jnp.float32)
    weights = mode_weight.astype(jnp.float32)
    grad_real = grad_hat[..., :modes_x].astype(jnp.float32)[None]
    grad_imag = grad_hat[..., modes_x:].astype(jnp.float32)[None]
    weight_real = weights[..., :modes_x]
    weight_imag = weights[..., modes_x:]
    back_real = jnp.sum(weight_real * grad_real + weight_imag * grad_imag, axis=1)
    back_imag = jnp.sum(weight_real * grad_imag - weight_imag * grad_real, axis=1)
    back_hat = jnp.concatenate([back_real, back_imag], axis=-1).astype(jnp.bfloat16)
    grid_rows = jnp.einsum(
        "cpr,rxq->pcxq", back_hat, x_inverse, preferred_element_type=jnp.float32
    ).astype(jnp.bfloat16)
    block = lax.all_to_all(grid_rows, "gx", split_axis=2, concat_axis=0, tiled=True)
    items = block.shape[1]
    plane = block.reshape(modes_y, modes_time, items, slab_cells, 2)
    joined = jnp.einsum(
        "jkcxa,ajyq->cxyqk", plane, plane_table, preferred_element_type=jnp.float32
    ).astype(jnp.bfloat16)
    spectral = jnp.dot(
        joined.reshape(-1, 2 * modes_time), inverse_time, preferred_element_type=jnp.float32
    )
    spectral_grad = scale_in * spectral.reshape(items, slab_cells, cells_y, cells_time)
    bypass = jnp.dot(
        bypass_weight, dz_field.reshape(channels, -1), preferred_element_type=jnp.float32
    ).reshape(dz_field.shape)
    input_grad = (spectral_grad + bypass).astype(jnp.bfloat16)[None]
    return (input_grad, mode_grad)


def host_tables(kept_count, length, two_sided):
    frequency = np.arange(kept_count)
    if two_sided:
        frequency = np.where(
            frequency < kept_count // 2, frequency, frequency + (length - kept_count)
        )
    product = frequency[:, None] * np.arange(length)[None, :] % length
    angle = product.astype(np.float32) * np.float32(2.0 * math.pi / length)
    return np.cos(angle).astype(np.float32), np.sin(angle).astype(np.float32)


def block_tables(sizes):
    ct, st = host_tables(sizes.modes_time, sizes.cells_time, False)
    cy, sy = host_tables(sizes.modes_y, sizes.cells_y, True)
    cx, sx = host_tables(sizes.modes_x, sizes.cells_x, True)
    group = np.eye(sizes.group, dtype=np.float32)
    slab = np.eye(sizes.slab, dtype=np.float32)
    rows = np.eye(sizes.rows, dtype=np.float32)
    time = np.stack([ct, -st])
    time_forward = np.einsum("cd,qkt->ctqdk", group, time)
    time_forward = time_forward.reshape(sizes.group * sizes.cells_time, -1)
    time_inverse = time_forward.T
    plane = np.stack([np.stack([cy, sy]), np.stack([-sy, cy])])
    plane = plane.reshape(2, 2, sizes.devices, sizes.rows, sizes.cells_y)
    y_forward = np.einsum("qpdjy,xz->djxqzpy", plane, slab)
    y_forward = y_forward.reshape(sizes.devices * sizes.piece, -1)
    y_inverse = y_forward.T
    x_table = np.stack(
        [np.concatenate([cx, -sx], 0).T, np.concatenate([sx, cx], 0).T], 1
    )
    x_table = x_table.reshape(-1, sizes.slab, 2, 2 * sizes.modes_x)
    real, imag = x_table[..., : sizes.modes_x], x_table[..., sizes.modes_x :]

    def x_rows(table):
        wide = np.einsum("gxqr,jl->gjxqlr", table, rows)
        return wide.reshape(-1, sizes.rows * table.shape[-1])

    x_input = x_rows(np.concatenate([real, real, imag, imag], -1))
    x_grad = x_rows(np.concatenate([real, imag, imag, -real], -1))
    x_inverse = x_rows(x_table)
    everything = (time_forward, time_inverse, y_forward, y_inverse, x_input, x_grad, x_inverse)
    return [table.astype(jnp.bfloat16) for table in everything]


class Sizes:
    def __init__(self, inputs, mode_weight, gx_count, sa_count):
        _, self.channels, self.slab, self.cells_y, self.cells_time = inputs
        self.modes_x = mode_weight[3] // 2
        self.modes_y, self.modes_time = MY, MT
        self.gx_count, self.sa_count = gx_count, sa_count
        self.devices = gx_count * sa_count
        self.cells_x = self.slab * gx_count
        self.pairs = self.modes_y * self.modes_time
        self.own_pairs = self.pairs // self.devices
        self.rows = self.own_pairs // self.modes_time
        self.piece = self.rows * self.slab * 2
        self.group = 128 // self.modes_time
        self.groups = self.channels // self.group
        cell_count = self.cells_x * self.cells_y * self.cells_time
        self.scale_in = float(self.modes_x * self.pairs * cell_count) ** (-0.25)
        self.scale_out = float(cell_count) ** (-0.5)

    def fits(self):
        return (
            self.own_pairs == self.rows * self.modes_time
            and self.own_pairs % 16 == 0
            and self.piece % 16 == 0
            and self.modes_x == 64
            and self.channels % self.group == 0
            and self.cells_time == 128
            and self.cells_y == 128
            and inputs_fit(self)
        )


def inputs_fit(sizes):
    return sizes.sa_count == 2 and sizes.channels == 16


def forward_kernel(
    sizes, inputs, preact, cotangent, time_forward, y_forward, dz, spectra, in_rows, dz_rows
):
    step = pl.program_id(0)
    slope = gelu_slope(preact[0, :, 0].astype(jnp.float32))
    gradient = (cotangent[0, :, 0].astype(jnp.float32) * slope).astype(jnp.bfloat16)
    dz[:, 0] = gradient
    first = pl.multiple_of(step * 2 * sizes.cells_y, 2 * sizes.cells_y)

    def time_rows(read, target):
        for cg in range(sizes.groups):
            left = jnp.concatenate(
                [read(cg * sizes.group + c) for c in range(sizes.group)], axis=1
            )
            both = jnp.dot(left, time_forward[...], preferred_element_type=jnp.float32)
            both = both.astype(jnp.bfloat16)
            for q in range(2):
                target[pl.ds(first + q * sizes.cells_y, sizes.cells_y), pl.ds(cg * 128, 128)] = (
                    both[:, q * 128 : (q + 1) * 128]
                )

    time_rows(lambda c: inputs[0, c, 0], in_rows)
    time_rows(lambda c: dz[c, 0], dz_rows)

    @pl.when(step == sizes.slab - 1)
    def _():
        for field, held in enumerate((in_rows, dz_rows)):
            plane = jnp.dot(y_forward[...], held[...], preferred_element_type=jnp.float32)
            plane = plane.astype(jnp.bfloat16)
            for cg in range(sizes.groups):
                spectra[:, field, cg] = plane[:, cg * 128 : (cg + 1) * 128].reshape(
                    sizes.devices, sizes.piece, 128
                )


def gelu_slope(values):
    return (
        0.5 * (1.0 + lax.erf(values * root_half))
        + values * jnp.exp(-0.5 * values * values) * gauss_norm
    )


def mode_kernel(
    sizes, spectra, weight, x_input, x_grad, x_inverse, mode_grad, rows_out, hats, back
):
    step = pl.program_id(0)
    samples, groups, kt = sizes.sa_count, sizes.groups, sizes.modes_time

    @pl.when(step == 0)
    def _():
        for field, table, scale in (
            (0, x_input, sizes.scale_in),
            (1, x_grad, sizes.scale_out),
        ):
            for s in range(samples):
                for cg in range(groups):
                    block = spectra[:, s, field, cg].reshape(-1, 128)
                    summed = lax.dot_general(
                        block, table[...], (((0,), (0,)), ((), ())),
                        preferred_element_type=jnp.float32,
                    )
                    summed = (scale * summed).astype(jnp.bfloat16).astype(jnp.float32)
                    for j in range(sizes.rows):
                        for part in range(2):
                            lanes = (2 * j + part) * 128
                            for c in range(sizes.group):
                                hats[
                                    2 * field + part, s, cg * sizes.group + c, pl.ds(j * kt, kt)
                                ] = summed[c * kt : (c + 1) * kt, lanes : lanes + 128]

    low = lax.broadcasted_iota(jnp.int32, (16, 128), 1) < sizes.modes_x
    cg, member = step // sizes.group, step % sizes.group
    for block in range(sizes.own_pairs // 16):
        rows = pl.ds(block * 16, 16)
        left = [[hats[part, s, step, rows] for s in range(samples)] for part in range(2)]
        total = [[None, None] for _ in range(samples)]
        for o in range(sizes.channels):
            right = [[hats[2 + part, s, o, rows] for s in range(samples)] for part in range(2)]
            value = weight[0, o, rows].astype(jnp.float32)
            grad = None
            for s in range(samples):
                for part in range(2):
                    term = left[part][s] * right[part][s]
                    grad = term if grad is None else grad + term
                    term = value * right[part][s]
                    held = total[s][part]
                    total[s][part] = term if held is None else held + term
            mode_grad[0, o, rows] = grad
        j, k = divmod(block * 16, kt)
        for s in range(samples):
            real, imag = total[s]
            real = real + pltpu.roll(real, sizes.modes_x, 1)
            imag = imag + pltpu.roll(imag, sizes.modes_x, 1)
            first = pl.multiple_of(member * kt + k, 16)
            back[s, cg, pl.ds(first, 16), pl.ds(j * 128, 128)] = jnp.where(
                low, real, imag
            ).astype(jnp.bfloat16)

    @pl.when(step == sizes.channels - 1)
    def _():
        for s in range(samples):
            for cg in range(groups):
                grid_rows = lax.dot_general(
                    x_inverse[...], back[s, cg], (((1,), (1,)), ((), ())),
                    preferred_element_type=jnp.float32,
                )
                rows_out[:, s, cg] = grid_rows.astype(jnp.bfloat16).reshape(
                    sizes.gx_count, sizes.piece, 128
                )


def inverse_kernel(
    sizes, grid_rows, dz, bypass, y_inverse, time_inverse, spread, input_grad, time_rows, mixer, acc
):
    step = pl.program_id(0)
    channels, group, cells_y = sizes.channels, sizes.group, sizes.cells_y

    @pl.when(step == 0)
    def _():
        joined = jnp.concatenate(
            [grid_rows[:, cg].reshape(-1, 128) for cg in range(sizes.groups)], axis=1
        )
        time_rows[...] = jnp.dot(
            y_inverse[...], joined, preferred_element_type=jnp.float32
        ).astype(jnp.bfloat16)
        tall = jnp.dot(spread[...], bypass[...], preferred_element_type=jnp.float32)
        wide = lax.dot_general(
            tall.astype(jnp.bfloat16), spread[...], (((1,), (1,)), ((), ())),
            preferred_element_type=jnp.float32,
        )
        row = lax.broadcasted_iota(jnp.int32, wide.shape, 0) % 16
        column = lax.broadcasted_iota(jnp.int32, wide.shape, 1) % 16
        mixer[...] = jnp.where(row == column, wide, 0.0).astype(jnp.bfloat16)

    first = pl.multiple_of(step * 2 * cells_y, 2 * cells_y)
    for cg in range(sizes.groups):
        lanes = pl.ds(cg * 128, 128)
        left = jnp.concatenate(
            [time_rows[pl.ds(first + q * cells_y, cells_y), lanes] for q in range(2)], axis=1
        )
        spectral = jnp.dot(left, time_inverse[...], preferred_element_type=jnp.float32)
        for c in range(group):
            acc[cg * group + c] = sizes.scale_in * spectral[:, c * 128 : (c + 1) * 128]
    for block in range(cells_y // 16):
        rows = pl.ds(block * 16, 16)
        mixed = jnp.dot(
            mixer[...], dz[:, 0, rows].reshape(-1, 128), preferred_element_type=jnp.float32
        ).reshape(channels, 16, 128)
        input_grad[0, :, 0, rows] = (mixed + acc[:, rows]).astype(jnp.bfloat16)


def whole(table):
    return pl.BlockSpec(table.shape, lambda *_: (0,) * table.ndim)


def shards(inputs, preact, cotangent, mode_weight, bypass_weight):
    sizes = Sizes(inputs.shape, mode_weight.shape, lax.axis_size("gx"), lax.axis_size("sa"))
    if not sizes.fits():
        return plain_shards(inputs, preact, cotangent, mode_weight, bypass_weight)
    tables_built = [jnp.asarray(table) for table in block_tables(sizes)]
    time_forward, time_inverse, y_forward, y_inverse, x_input, x_grad, x_inverse = tables_built
    channels, slab, cells_y, cells_time = inputs.shape[1:]
    params = pltpu.CompilerParams(vmem_limit_bytes=48 * 2**20)
    field_block = pl.BlockSpec(
        (1, channels, 1, cells_y, cells_time), lambda x: (0, 0, x, 0, 0)
    )
    dz_block = pl.BlockSpec((channels, 1, cells_y, cells_time), lambda x: (0, x, 0, 0))
    packet = (sizes.devices, 2, sizes.groups, sizes.piece, 128)
    rows_shape = (2 * slab * cells_y, sizes.groups * 128)
    dz, spectra = pl.pallas_call(
        functools.partial(forward_kernel, sizes),
        grid=(slab,),
        in_specs=[field_block] * 3 + [whole(time_forward), whole(y_forward)],
        out_specs=[dz_block, pl.BlockSpec(packet, lambda x: (0,) * 5)],
        out_shape=[
            jax.ShapeDtypeStruct(inputs.shape[1:], jnp.bfloat16),
            jax.ShapeDtypeStruct(packet, jnp.bfloat16),
        ],
        scratch_shapes=[pltpu.VMEM(rows_shape, jnp.bfloat16)] * 2,
        compiler_params=params,
        name="forward",
    )(inputs, preact, cotangent, time_forward, y_forward)
    spectra = lax.all_to_all(spectra, ("gx", "sa"), split_axis=0, concat_axis=0, tiled=True)
    spectra = spectra.reshape((sizes.gx_count, sizes.sa_count) + packet[1:])
    own = sizes.own_pairs
    out_packet = (sizes.gx_count, sizes.sa_count, sizes.groups, sizes.piece, 128)
    mode_grad, grid_rows = pl.pallas_call(
        functools.partial(mode_kernel, sizes),
        grid=(channels,),
        in_specs=[
            whole(spectra),
            pl.BlockSpec(
                (1, channels, own, 128), lambda i: (i, 0, lax.axis_index("sa"), 0)
            ),
            whole(x_input),
            whole(x_grad),
            whole(x_inverse),
        ],
        out_specs=[
            pl.BlockSpec((1, channels, own, 128), lambda i: (i, 0, 0, 0)),
            pl.BlockSpec(out_packet, lambda i: (0,) * 5),
        ],
        out_shape=[
            jax.ShapeDtypeStruct((channels, channels, own, 128), jnp.float32),
            jax.ShapeDtypeStruct(out_packet, jnp.bfloat16),
        ],
        scratch_shapes=[
            pltpu.VMEM((4, sizes.sa_count, channels, own, 128), jnp.float32),
            pltpu.VMEM((sizes.sa_count, sizes.groups, 128, sizes.rows * 128), jnp.bfloat16),
        ],
        compiler_params=params,
        name="modes",
    )(spectra, mode_weight, x_input, x_grad, x_inverse)
    grid_rows = lax.all_to_all(
        grid_rows.reshape((sizes.devices,) + out_packet[2:]),
        ("gx", "sa"), split_axis=0, concat_axis=0, tiled=True,
    )
    spread = jnp.asarray(np.repeat(np.eye(channels), 16, axis=0).astype(jnp.bfloat16))
    input_grad = pl.pallas_call(
        functools.partial(inverse_kernel, sizes),
        grid=(slab,),
        in_specs=[
            whole(grid_rows), dz_block, whole(bypass_weight), whole(y_inverse),
            whole(time_inverse), whole(spread),
        ],
        out_specs=field_block,
        out_shape=jax.ShapeDtypeStruct(inputs.shape, jnp.bfloat16),
        scratch_shapes=[
            pltpu.VMEM(rows_shape, jnp.bfloat16),
            pltpu.VMEM((channels * 16, channels * 16), jnp.bfloat16),
            pltpu.VMEM((channels, cells_y, cells_time), jnp.float32),
        ],
        compiler_params=params,
        name="inverse",
    )(grid_rows, dz, bypass_weight, y_inverse, time_inverse, spread)
    return input_grad, mode_grad


def solution(mesh):
    placed = (
        P("sa", None, "gx", None, None),
        P("sa", None, "gx", None, None),
        P("sa", None, "gx", None, None),
        P(None, None, "gx", None),
        P(),
    )
    return jax.shard_map(
        shards,
        mesh=mesh,
        in_specs=placed,
        out_specs=(P("sa", None, "gx", None, None), P(None, None, ("gx", "sa"), None)),
        check_vma=False,
    )
```

```python
import functools
import math

import jax
import jax.numpy as jnp
import numpy as np
from jax import lax
from jax.experimental import pallas as pl
from jax.experimental.pallas import tpu as pltpu
from jax.sharding import PartitionSpec as P

MY = 64
MT = 32


root_half = math.sqrt(0.5)
gauss_norm = 1.0 / math.sqrt(2.0 * math.pi)


def tables(kept_count, length, two_sided):
    frequency = jnp.arange(kept_count, dtype=jnp.int32)
    if two_sided:
        frequency = jnp.where(
            frequency < kept_count // 2, frequency, frequency + (length - kept_count)
        )
    position = jnp.arange(length, dtype=jnp.int32)
    product = frequency[:, None] * position[None, :] % length
    phase_angle = product.astype(jnp.float32) * (2.0 * math.pi / length)
    return (jnp.cos(phase_angle).astype(jnp.bfloat16), jnp.sin(phase_angle).astype(jnp.bfloat16))


def gelu_backward(preact_block, cotangent_block):
    values = preact_block.astype(jnp.float32)
    slope = (
        0.5 * (1.0 + jax.scipy.special.erf(values * root_half))
        + values * jnp.exp(-0.5 * values * values) * gauss_norm
    )
    return (cotangent_block.astype(jnp.float32) * slope).astype(jnp.bfloat16)


def gradient_term(input_hat, grad_hat, half):
    input_real = input_hat[..., :half].astype(jnp.float32)[:, None]
    input_imag = input_hat[..., half:].astype(jnp.float32)[:, None]
    grad_real = grad_hat[..., :half].astype(jnp.float32)[None]
    grad_imag = grad_hat[..., half:].astype(jnp.float32)[None]
    return jnp.concatenate(
        [
            input_real * grad_real + input_imag * grad_imag,
            input_real * grad_imag - input_imag * grad_real,
        ],
        axis=-1,
    )


def plain_shards(inputs, preact, cotangent, mode_weight, bypass_weight):
    channels = inputs.shape[1]
    slab_cells = inputs.shape[2]
    cells_y = inputs.shape[3]
    cells_time = inputs.shape[4]
    devices_x = lax.axis_size("gx")
    cells_x = slab_cells * devices_x
    modes_x = mode_weight.shape[3] // 2
    modes_y = MY
    modes_time = MT
    pair_count = modes_y * modes_time
    cell_count = cells_x * cells_y * cells_time
    scale_in = float(modes_x * pair_count * cell_count) ** (-0.25)
    scale_out = float(cell_count) ** (-0.5)
    cosine_time, sine_time = tables(modes_time, cells_time, False)
    cosine_y, sine_y = tables(modes_y, cells_y, True)
    cosine_x, sine_x = tables(modes_x, cells_x, True)
    forward_time = jnp.concatenate([cosine_time.T, -sine_time.T], axis=1)
    inverse_time = jnp.concatenate([cosine_time, -sine_time], axis=0)
    plane_table = jnp.stack([jnp.stack([cosine_y, sine_y], -1), jnp.stack([-sine_y, cosine_y], -1)])
    x_forward = jnp.stack(
        [jnp.concatenate([cosine_x, -sine_x], 0).T, jnp.concatenate([sine_x, cosine_x], 0).T], 1
    )
    x_inverse = jnp.stack(
        [jnp.concatenate([cosine_x, -sine_x], 0), jnp.concatenate([sine_x, cosine_x], 0)], -1
    )

    def spectra(field):
        sectioned = jnp.dot(
            field.reshape(-1, cells_time), forward_time, preferred_element_type=jnp.float32
        ).astype(jnp.bfloat16)
        sectioned = sectioned.reshape(channels, slab_cells, cells_y, 2, modes_time)
        plane = jnp.einsum(
            "cxyqk,ajyq->jkcxa", sectioned, plane_table, preferred_element_type=jnp.float32
        ).astype(jnp.bfloat16)
        return plane.reshape(pair_count, channels, slab_cells, 2)

    def x_transform(block, factor):
        summed = jnp.einsum("pcxq,xqr->cpr", block, x_forward, preferred_element_type=jnp.float32)
        return (factor * summed).astype(jnp.bfloat16)

    dz_field = gelu_backward(preact[0], cotangent[0])
    input_hat = x_transform(
        lax.all_to_all(spectra(inputs[0]), "gx", split_axis=0, concat_axis=2, tiled=True), scale_in
    )
    grad_hat = x_transform(
        lax.all_to_all(spectra(dz_field), "gx", split_axis=0, concat_axis=2, tiled=True), scale_out
    )
    mode_grad = lax.psum_scatter(
        gradient_term(input_hat, grad_hat, modes_x).astype(jnp.bfloat16),
        "sa",
        scatter_dimension=2,
        tiled=True,
    ).astype(jnp.float32)
    weights = mode_weight.astype(jnp.float32)
    grad_real = grad_hat[..., :modes_x].astype(jnp.float32)[None]
    grad_imag = grad_hat[..., modes_x:].astype(jnp.float32)[None]
    weight_real = weights[..., :modes_x]
    weight_imag = weights[..., modes_x:]
    back_real = jnp.sum(weight_real * grad_real + weight_imag * grad_imag, axis=1)
    back_imag = jnp.sum(weight_real * grad_imag - weight_imag * grad_real, axis=1)
    back_hat = jnp.concatenate([back_real, back_imag], axis=-1).astype(jnp.bfloat16)
    grid_rows = jnp.einsum(
        "cpr,rxq->pcxq", back_hat, x_inverse, preferred_element_type=jnp.float32
    ).astype(jnp.bfloat16)
    block = lax.all_to_all(grid_rows, "gx", split_axis=2, concat_axis=0, tiled=True)
    items = block.shape[1]
    plane = block.reshape(modes_y, modes_time, items, slab_cells, 2)
    joined = jnp.einsum(
        "jkcxa,ajyq->cxyqk", plane, plane_table, preferred_element_type=jnp.float32
    ).astype(jnp.bfloat16)
    spectral = jnp.dot(
        joined.reshape(-1, 2 * modes_time), inverse_time, preferred_element_type=jnp.float32
    )
    spectral_grad = scale_in * spectral.reshape(items, slab_cells, cells_y, cells_time)
    bypass = jnp.dot(
        bypass_weight, dz_field.reshape(channels, -1), preferred_element_type=jnp.float32
    ).reshape(dz_field.shape)
    input_grad = (spectral_grad + bypass).astype(jnp.bfloat16)[None]
    return (input_grad, mode_grad)


def host_tables(kept_count, length, two_sided):
    frequency = np.arange(kept_count)
    if two_sided:
        frequency = np.where(
            frequency < kept_count // 2, frequency, frequency + (length - kept_count)
        )
    product = frequency[:, None] * np.arange(length)[None, :] % length
    angle = product.astype(np.float32) * np.float32(2.0 * math.pi / length)
    return np.cos(angle).astype(np.float32), np.sin(angle).astype(np.float32)


def block_tables(sizes):
    ct, st = host_tables(sizes.modes_time, sizes.cells_time, False)
    cy, sy = host_tables(sizes.modes_y, sizes.cells_y, True)
    cx, sx = host_tables(sizes.modes_x, sizes.cells_x, True)
    group = np.eye(sizes.group, dtype=np.float32)
    slab = np.eye(sizes.slab, dtype=np.float32)
    rows = np.eye(sizes.rows, dtype=np.float32)
    time = np.stack([ct, -st])
    time_forward = np.einsum("cd,qkt->ctqdk", group, time)
    time_forward = time_forward.reshape(sizes.group * sizes.cells_time, -1)
    time_inverse = time_forward.T
    plane = np.stack([np.stack([cy, sy]), np.stack([-sy, cy])])
    plane = plane.reshape(2, 2, sizes.devices, sizes.rows, sizes.cells_y)
    y_forward = np.einsum("qpdjy,xz->djxqzpy", plane, slab)
    y_forward = y_forward.reshape(sizes.devices * sizes.piece, -1)
    y_inverse = y_forward.T
    x_table = np.stack(
        [np.concatenate([cx, -sx], 0).T, np.concatenate([sx, cx], 0).T], 1
    )
    x_table = x_table.reshape(-1, sizes.slab, 2, 2 * sizes.modes_x)
    real, imag = x_table[..., : sizes.modes_x], x_table[..., sizes.modes_x :]

    def x_rows(table):
        wide = np.einsum("gxqr,jl->gjxqlr", table, rows)
        return wide.reshape(-1, sizes.rows * table.shape[-1])

    x_input = x_rows(np.concatenate([real, real, imag, imag], -1))
    x_grad = x_rows(np.concatenate([real, imag, imag, -real], -1))
    x_inverse = x_rows(x_table)
    everything = (time_forward, time_inverse, y_forward, y_inverse, x_input, x_grad, x_inverse)
    return [table.astype(jnp.bfloat16) for table in everything]


class Sizes:
    def __init__(self, inputs, mode_weight, gx_count, sa_count):
        _, self.channels, self.slab, self.cells_y, self.cells_time = inputs
        self.modes_x = mode_weight[3] // 2
        self.modes_y, self.modes_time = MY, MT
        self.gx_count, self.sa_count = gx_count, sa_count
        self.devices = gx_count * sa_count
        self.cells_x = self.slab * gx_count
        self.pairs = self.modes_y * self.modes_time
        self.own_pairs = self.pairs // self.devices
        self.rows = self.own_pairs // self.modes_time
        self.piece = self.rows * self.slab * 2
        self.group = 128 // self.modes_time
        self.groups = self.channels // self.group
        cell_count = self.cells_x * self.cells_y * self.cells_time
        self.scale_in = float(self.modes_x * self.pairs * cell_count) ** (-0.25)
        self.scale_out = float(cell_count) ** (-0.5)

    def fits(self):
        return (
            self.own_pairs == self.rows * self.modes_time
            and self.own_pairs % 16 == 0
            and self.piece % 16 == 0
            and self.modes_x == 64
            and self.channels % self.group == 0
            and self.cells_time == 128
            and self.cells_y == 128
            and inputs_fit(self)
        )


def inputs_fit(sizes):
    return sizes.sa_count == 2 and sizes.channels == 16


def forward_kernel(
    sizes, inputs, preact, cotangent, time_forward, y_forward, dz, spectra, in_rows, dz_rows
):
    step = pl.program_id(0)
    slope = gelu_slope(preact[0, :, 0].astype(jnp.float32))
    gradient = (cotangent[0, :, 0].astype(jnp.float32) * slope).astype(jnp.bfloat16)
    dz[:, 0] = gradient
    first = pl.multiple_of(step * 2 * sizes.cells_y, 2 * sizes.cells_y)

    def time_rows(read, target):
        for cg in range(sizes.groups):
            left = jnp.concatenate(
                [read(cg * sizes.group + c) for c in range(sizes.group)], axis=1
            )
            both = jnp.dot(left, time_forward[...], preferred_element_type=jnp.float32)
            both = both.astype(jnp.bfloat16)
            for q in range(2):
                target[pl.ds(first + q * sizes.cells_y, sizes.cells_y), pl.ds(cg * 128, 128)] = (
                    both[:, q * 128 : (q + 1) * 128]
                )

    time_rows(lambda c: inputs[0, c, 0], in_rows)
    time_rows(lambda c: dz[c, 0], dz_rows)

    @pl.when(step == sizes.slab - 1)
    def _():
        for field, held in enumerate((in_rows, dz_rows)):
            plane = jnp.dot(y_forward[...], held[...], preferred_element_type=jnp.float32)
            plane = plane.astype(jnp.bfloat16)
            for cg in range(sizes.groups):
                spectra[:, field, cg] = plane[:, cg * 128 : (cg + 1) * 128].reshape(
                    sizes.devices, sizes.piece, 128
                )


def gelu_slope(values):
    return (
        0.5 * (1.0 + lax.erf(values * root_half))
        + values * jnp.exp(-0.5 * values * values) * gauss_norm
    )


def mode_kernel(
    sizes, spectra, weight, x_input, x_grad, x_inverse, mode_grad, rows_out, hats, back
):
    step = pl.program_id(0)
    samples, groups, kt = sizes.sa_count, sizes.groups, sizes.modes_time

    @pl.when(step == 0)
    def _():
        for field, table, scale in (
            (0, x_input, sizes.scale_in),
            (1, x_grad, sizes.scale_out),
        ):
            for s in range(samples):
                for cg in range(groups):
                    block = spectra[:, s, field, cg].reshape(-1, 128)
                    summed = lax.dot_general(
                        block, table[...], (((0,), (0,)), ((), ())),
                        preferred_element_type=jnp.float32,
                    )
                    summed = (scale * summed).astype(jnp.bfloat16).astype(jnp.float32)
                    for j in range(sizes.rows):
                        for part in range(2):
                            lanes = (2 * j + part) * 128
                            for c in range(sizes.group):
                                hats[
                                    2 * field + part, s, cg * sizes.group + c, pl.ds(j * kt, kt)
                                ] = summed[c * kt : (c + 1) * kt, lanes : lanes + 128]

    low = lax.broadcasted_iota(jnp.int32, (16, 128), 1) < sizes.modes_x
    cg, member = step // sizes.group, step % sizes.group
    for block in range(sizes.own_pairs // 16):
        rows = pl.ds(block * 16, 16)
        left = [[hats[part, s, step, rows] for s in range(samples)] for part in range(2)]
        total = [[None, None] for _ in range(samples)]
        for o in range(sizes.channels):
            right = [[hats[2 + part, s, o, rows] for s in range(samples)] for part in range(2)]
            value = weight[0, o, rows].astype(jnp.float32)
            grad = None
            for s in range(samples):
                for part in range(2):
                    term = left[part][s] * right[part][s]
                    grad = term if grad is None else grad + term
                    term = value * right[part][s]
                    held = total[s][part]
                    total[s][part] = term if held is None else held + term
            mode_grad[0, o, rows] = grad
        j, k = divmod(block * 16, kt)
        for s in range(samples):
            real, imag = total[s]
            real = real + pltpu.roll(real, sizes.modes_x, 1)
            imag = imag + pltpu.roll(imag, sizes.modes_x, 1)
            first = pl.multiple_of(member * kt + k, 16)
            back[s, cg, pl.ds(first, 16), pl.ds(j * 128, 128)] = jnp.where(
                low, real, imag
            ).astype(jnp.bfloat16)

    @pl.when(step == sizes.channels - 1)
    def _():
        for s in range(samples):
            for cg in range(groups):
                grid_rows = lax.dot_general(
                    x_inverse[...], back[s, cg], (((1,), (1,)), ((), ())),
                    preferred_element_type=jnp.float32,
                )
                rows_out[:, s, cg] = grid_rows.astype(jnp.bfloat16).reshape(
                    sizes.gx_count, sizes.piece, 128
                )


def inverse_kernel(
    sizes, grid_rows, dz, bypass, y_inverse, time_inverse, spread, input_grad, time_rows, mixer, acc
):
    step = pl.program_id(0)
    channels, group, cells_y = sizes.channels, sizes.group, sizes.cells_y

    @pl.when(step == 0)
    def _():
        joined = jnp.concatenate(
            [grid_rows[:, cg].reshape(-1, 128) for cg in range(sizes.groups)], axis=1
        )
        time_rows[...] = jnp.dot(
            y_inverse[...], joined, preferred_element_type=jnp.float32
        ).astype(jnp.bfloat16)
        tall = jnp.dot(spread[...], bypass[...], preferred_element_type=jnp.float32)
        wide = lax.dot_general(
            tall.astype(jnp.bfloat16), spread[...], (((1,), (1,)), ((), ())),
            preferred_element_type=jnp.float32,
        )
        row = lax.broadcasted_iota(jnp.int32, wide.shape, 0) % 16
        column = lax.broadcasted_iota(jnp.int32, wide.shape, 1) % 16
        mixer[...] = jnp.where(row == column, wide, 0.0).astype(jnp.bfloat16)

    first = pl.multiple_of(step * 2 * cells_y, 2 * cells_y)
    for cg in range(sizes.groups):
        lanes = pl.ds(cg * 128, 128)
        left = jnp.concatenate(
            [time_rows[pl.ds(first + q * cells_y, cells_y), lanes] for q in range(2)], axis=1
        )
        spectral = jnp.dot(left, time_inverse[...], preferred_element_type=jnp.float32)
        for c in range(group):
            acc[cg * group + c] = sizes.scale_in * spectral[:, c * 128 : (c + 1) * 128]
    for block in range(cells_y // 16):
        rows = pl.ds(block * 16, 16)
        mixed = jnp.dot(
            mixer[...], dz[:, 0, rows].reshape(-1, 128), preferred_element_type=jnp.float32
        ).reshape(channels, 16, 128)
        input_grad[0, :, 0, rows] = (mixed + acc[:, rows]).astype(jnp.bfloat16)


def exchange_kernel(gx_count, sa_count, packet, landed, send_sem, recv_sem, own_sem):
    devices = gx_count * sa_count
    me = lax.axis_index("gx") * sa_count + lax.axis_index("sa")

    def place(other):
        return (other // sa_count, other % sa_count)

    barrier = pltpu.get_barrier_semaphore()

    @pl.loop(1, devices)
    def _(step):
        pl.semaphore_signal(
            barrier, inc=1, device_id=place((me + step) % devices),
            device_id_type=pl.DeviceIdType.MESH,
        )

    own = pltpu.make_async_copy(packet.at[me], landed.at[me], own_sem)
    own.start()
    pl.semaphore_wait(barrier, devices - 1)

    def copy(step):
        other = (me + step) % devices
        return pltpu.make_async_remote_copy(
            src_ref=packet.at[other],
            dst_ref=landed.at[me],
            send_sem=send_sem.at[step],
            recv_sem=recv_sem.at[step],
            device_id=place(other),
            device_id_type=pl.DeviceIdType.MESH,
        )

    @pl.loop(1, devices)
    def _(step):
        copy(step).start()

    own.wait()

    @pl.loop(1, devices)
    def _(step):
        copy(step).wait()


def exchange(packet, sizes, collective_id):
    count = sizes.devices
    return pl.pallas_call(
        functools.partial(exchange_kernel, sizes.gx_count, sizes.sa_count),
        in_specs=[pl.BlockSpec(memory_space=pltpu.VMEM)],
        out_specs=pl.BlockSpec(memory_space=pltpu.VMEM),
        out_shape=jax.ShapeDtypeStruct(packet.shape, packet.dtype),
        scratch_shapes=[
            pltpu.SemaphoreType.DMA((count,)),
            pltpu.SemaphoreType.DMA((count,)),
            pltpu.SemaphoreType.DMA(()),
        ],
        compiler_params=pltpu.CompilerParams(
            collective_id=collective_id, has_side_effects=True
        ),
        name="exchange",
    )(packet)


def whole(table):
    return pl.BlockSpec(table.shape, lambda *_: (0,) * table.ndim)


def shards(inputs, preact, cotangent, mode_weight, bypass_weight):
    sizes = Sizes(inputs.shape, mode_weight.shape, lax.axis_size("gx"), lax.axis_size("sa"))
    if not sizes.fits():
        return plain_shards(inputs, preact, cotangent, mode_weight, bypass_weight)
    tables_built = [jnp.asarray(table) for table in block_tables(sizes)]
    time_forward, time_inverse, y_forward, y_inverse, x_input, x_grad, x_inverse = tables_built
    channels, slab, cells_y, cells_time = inputs.shape[1:]
    params = pltpu.CompilerParams(vmem_limit_bytes=48 * 2**20)
    field_block = pl.BlockSpec(
        (1, channels, 1, cells_y, cells_time), lambda x: (0, 0, x, 0, 0)
    )
    dz_block = pl.BlockSpec((channels, 1, cells_y, cells_time), lambda x: (0, x, 0, 0))
    packet = (sizes.devices, 2, sizes.groups, sizes.piece, 128)
    rows_shape = (2 * slab * cells_y, sizes.groups * 128)
    dz, spectra = pl.pallas_call(
        functools.partial(forward_kernel, sizes),
        grid=(slab,),
        in_specs=[field_block] * 3 + [whole(time_forward), whole(y_forward)],
        out_specs=[dz_block, pl.BlockSpec(packet, lambda x: (0,) * 5)],
        out_shape=[
            jax.ShapeDtypeStruct(inputs.shape[1:], jnp.bfloat16),
            jax.ShapeDtypeStruct(packet, jnp.bfloat16),
        ],
        scratch_shapes=[pltpu.VMEM(rows_shape, jnp.bfloat16)] * 2,
        compiler_params=params,
        name="forward",
    )(inputs, preact, cotangent, time_forward, y_forward)
    spectra = exchange(spectra, sizes, 0)
    spectra = spectra.reshape((sizes.gx_count, sizes.sa_count) + packet[1:])
    own = sizes.own_pairs
    out_packet = (sizes.gx_count, sizes.sa_count, sizes.groups, sizes.piece, 128)
    mode_grad, grid_rows = pl.pallas_call(
        functools.partial(mode_kernel, sizes),
        grid=(channels,),
        in_specs=[
            whole(spectra),
            pl.BlockSpec(
                (1, channels, own, 128), lambda i: (i, 0, lax.axis_index("sa"), 0)
            ),
            whole(x_input),
            whole(x_grad),
            whole(x_inverse),
        ],
        out_specs=[
            pl.BlockSpec((1, channels, own, 128), lambda i: (i, 0, 0, 0)),
            pl.BlockSpec(out_packet, lambda i: (0,) * 5),
        ],
        out_shape=[
            jax.ShapeDtypeStruct((channels, channels, own, 128), jnp.float32),
            jax.ShapeDtypeStruct(out_packet, jnp.bfloat16),
        ],
        scratch_shapes=[
            pltpu.VMEM((4, sizes.sa_count, channels, own, 128), jnp.float32),
            pltpu.VMEM((sizes.sa_count, sizes.groups, 128, sizes.rows * 128), jnp.bfloat16),
        ],
        compiler_params=params,
        name="modes",
    )(spectra, mode_weight, x_input, x_grad, x_inverse)
    grid_rows = exchange(grid_rows.reshape((sizes.devices,) + out_packet[2:]), sizes, 1)
    spread = jnp.asarray(np.repeat(np.eye(channels), 16, axis=0).astype(jnp.bfloat16))
    input_grad = pl.pallas_call(
        functools.partial(inverse_kernel, sizes),
        grid=(slab,),
        in_specs=[
            whole(grid_rows), dz_block, whole(bypass_weight), whole(y_inverse),
            whole(time_inverse), whole(spread),
        ],
        out_specs=field_block,
        out_shape=jax.ShapeDtypeStruct(inputs.shape, jnp.bfloat16),
        scratch_shapes=[
            pltpu.VMEM(rows_shape, jnp.bfloat16),
            pltpu.VMEM((channels * 16, channels * 16), jnp.bfloat16),
            pltpu.VMEM((channels, cells_y, cells_time), jnp.float32),
        ],
        compiler_params=params,
        name="inverse",
    )(grid_rows, dz, bypass_weight, y_inverse, time_inverse, spread)
    return input_grad, mode_grad


def solution(mesh):
    placed = (
        P("sa", None, "gx", None, None),
        P("sa", None, "gx", None, None),
        P("sa", None, "gx", None, None),
        P(None, None, "gx", None),
        P(),
    )
    return jax.shard_map(
        shards,
        mesh=mesh,
        in_specs=placed,
        out_specs=(P("sa", None, "gx", None, None), P(None, None, ("gx", "sa"), None)),
        check_vma=False,
    )
```

```python
import functools
import math

import jax
import jax.numpy as jnp
import numpy as np
from jax import lax
from jax.experimental import pallas as pl
from jax.experimental.pallas import tpu as pltpu
from jax.sharding import PartitionSpec as P

MY = 64
MT = 32
VMEM_BYTES = 60 * 2**20


root_half = math.sqrt(0.5)
gauss_norm = 1.0 / math.sqrt(2.0 * math.pi)


def tables(kept_count, length, two_sided):
    frequency = jnp.arange(kept_count, dtype=jnp.int32)
    if two_sided:
        frequency = jnp.where(
            frequency < kept_count // 2, frequency, frequency + (length - kept_count)
        )
    position = jnp.arange(length, dtype=jnp.int32)
    product = frequency[:, None] * position[None, :] % length
    phase_angle = product.astype(jnp.float32) * (2.0 * math.pi / length)
    return (jnp.cos(phase_angle).astype(jnp.bfloat16), jnp.sin(phase_angle).astype(jnp.bfloat16))


def gelu_backward(preact_block, cotangent_block):
    values = preact_block.astype(jnp.float32)
    slope = (
        0.5 * (1.0 + jax.scipy.special.erf(values * root_half))
        + values * jnp.exp(-0.5 * values * values) * gauss_norm
    )
    return (cotangent_block.astype(jnp.float32) * slope).astype(jnp.bfloat16)


def gradient_term(input_hat, grad_hat, half):
    input_real = input_hat[..., :half].astype(jnp.float32)[:, None]
    input_imag = input_hat[..., half:].astype(jnp.float32)[:, None]
    grad_real = grad_hat[..., :half].astype(jnp.float32)[None]
    grad_imag = grad_hat[..., half:].astype(jnp.float32)[None]
    return jnp.concatenate(
        [
            input_real * grad_real + input_imag * grad_imag,
            input_real * grad_imag - input_imag * grad_real,
        ],
        axis=-1,
    )


def plain_shards(inputs, preact, cotangent, mode_weight, bypass_weight):
    channels = inputs.shape[1]
    slab_cells = inputs.shape[2]
    cells_y = inputs.shape[3]
    cells_time = inputs.shape[4]
    devices_x = lax.axis_size("gx")
    cells_x = slab_cells * devices_x
    modes_x = mode_weight.shape[3] // 2
    modes_y = MY
    modes_time = MT
    pair_count = modes_y * modes_time
    cell_count = cells_x * cells_y * cells_time
    scale_in = float(modes_x * pair_count * cell_count) ** (-0.25)
    scale_out = float(cell_count) ** (-0.5)
    cosine_time, sine_time = tables(modes_time, cells_time, False)
    cosine_y, sine_y = tables(modes_y, cells_y, True)
    cosine_x, sine_x = tables(modes_x, cells_x, True)
    forward_time = jnp.concatenate([cosine_time.T, -sine_time.T], axis=1)
    inverse_time = jnp.concatenate([cosine_time, -sine_time], axis=0)
    plane_table = jnp.stack([jnp.stack([cosine_y, sine_y], -1), jnp.stack([-sine_y, cosine_y], -1)])
    x_forward = jnp.stack(
        [jnp.concatenate([cosine_x, -sine_x], 0).T, jnp.concatenate([sine_x, cosine_x], 0).T], 1
    )
    x_inverse = jnp.stack(
        [jnp.concatenate([cosine_x, -sine_x], 0), jnp.concatenate([sine_x, cosine_x], 0)], -1
    )

    def spectra(field):
        sectioned = jnp.dot(
            field.reshape(-1, cells_time), forward_time, preferred_element_type=jnp.float32
        ).astype(jnp.bfloat16)
        sectioned = sectioned.reshape(channels, slab_cells, cells_y, 2, modes_time)
        plane = jnp.einsum(
            "cxyqk,ajyq->jkcxa", sectioned, plane_table, preferred_element_type=jnp.float32
        ).astype(jnp.bfloat16)
        return plane.reshape(pair_count, channels, slab_cells, 2)

    def x_transform(block, factor):
        summed = jnp.einsum("pcxq,xqr->cpr", block, x_forward, preferred_element_type=jnp.float32)
        return (factor * summed).astype(jnp.bfloat16)

    dz_field = gelu_backward(preact[0], cotangent[0])
    input_hat = x_transform(
        lax.all_to_all(spectra(inputs[0]), "gx", split_axis=0, concat_axis=2, tiled=True), scale_in
    )
    grad_hat = x_transform(
        lax.all_to_all(spectra(dz_field), "gx", split_axis=0, concat_axis=2, tiled=True), scale_out
    )
    mode_grad = lax.psum_scatter(
        gradient_term(input_hat, grad_hat, modes_x).astype(jnp.bfloat16),
        "sa",
        scatter_dimension=2,
        tiled=True,
    ).astype(jnp.float32)
    weights = mode_weight.astype(jnp.float32)
    grad_real = grad_hat[..., :modes_x].astype(jnp.float32)[None]
    grad_imag = grad_hat[..., modes_x:].astype(jnp.float32)[None]
    weight_real = weights[..., :modes_x]
    weight_imag = weights[..., modes_x:]
    back_real = jnp.sum(weight_real * grad_real + weight_imag * grad_imag, axis=1)
    back_imag = jnp.sum(weight_real * grad_imag - weight_imag * grad_real, axis=1)
    back_hat = jnp.concatenate([back_real, back_imag], axis=-1).astype(jnp.bfloat16)
    grid_rows = jnp.einsum(
        "cpr,rxq->pcxq", back_hat, x_inverse, preferred_element_type=jnp.float32
    ).astype(jnp.bfloat16)
    block = lax.all_to_all(grid_rows, "gx", split_axis=2, concat_axis=0, tiled=True)
    items = block.shape[1]
    plane = block.reshape(modes_y, modes_time, items, slab_cells, 2)
    joined = jnp.einsum(
        "jkcxa,ajyq->cxyqk", plane, plane_table, preferred_element_type=jnp.float32
    ).astype(jnp.bfloat16)
    spectral = jnp.dot(
        joined.reshape(-1, 2 * modes_time), inverse_time, preferred_element_type=jnp.float32
    )
    spectral_grad = scale_in * spectral.reshape(items, slab_cells, cells_y, cells_time)
    bypass = jnp.dot(
        bypass_weight, dz_field.reshape(channels, -1), preferred_element_type=jnp.float32
    ).reshape(dz_field.shape)
    input_grad = (spectral_grad + bypass).astype(jnp.bfloat16)[None]
    return (input_grad, mode_grad)


def host_tables(kept_count, length, two_sided):
    frequency = np.arange(kept_count)
    if two_sided:
        frequency = np.where(
            frequency < kept_count // 2, frequency, frequency + (length - kept_count)
        )
    product = frequency[:, None] * np.arange(length)[None, :] % length
    angle = product.astype(np.float32) * np.float32(2.0 * math.pi / length)
    return np.cos(angle).astype(np.float32), np.sin(angle).astype(np.float32)


def block_tables(sizes):
    ct, st = host_tables(sizes.modes_time, sizes.cells_time, False)
    cy, sy = host_tables(sizes.modes_y, sizes.cells_y, True)
    cx, sx = host_tables(sizes.modes_x, sizes.cells_x, True)
    group = np.eye(sizes.group, dtype=np.float32)
    rows = np.eye(sizes.rows, dtype=np.float32)
    time = np.stack([ct, -st])
    time_forward = np.einsum("cd,qkt->ctqdk", group, time)
    time_forward = time_forward.reshape(sizes.group * sizes.cells_time, -1)
    time_inverse = time_forward.T
    plane = np.stack([np.stack([cy, sy]), np.stack([-sy, cy])])
    plane = plane.reshape(2, 2, sizes.devices, sizes.rows, sizes.cells_y)
    plane = np.einsum("qpdjy->djqpy", plane)
    y_forward = plane.reshape(2 * sizes.modes_y, -1)
    y_inverse = y_forward.T
    x_table = np.stack(
        [np.concatenate([cx, -sx], 0).T, np.concatenate([sx, cx], 0).T], 1
    )
    x_table = x_table.reshape(-1, sizes.slab, 2, 2 * sizes.modes_x)
    real, imag = x_table[..., : sizes.modes_x], x_table[..., sizes.modes_x :]

    def x_rows(table):
        wide = np.einsum("gxqr,jl->gjxqlr", table, rows)
        return wide.reshape(-1, sizes.rows * table.shape[-1])

    x_input = x_rows(np.concatenate([real, real, imag, imag], -1))
    x_grad = x_rows(np.concatenate([real, imag, imag, -real], -1))
    x_inverse = x_rows(x_table)
    everything = (time_forward, time_inverse, y_forward, y_inverse, x_input, x_grad, x_inverse)
    return [table.astype(jnp.bfloat16) for table in everything]


class Sizes:
    def __init__(self, inputs, mode_weight, gx_count, sa_count):
        _, self.channels, self.slab, self.cells_y, self.cells_time = inputs
        self.modes_x = mode_weight[3] // 2
        self.modes_y, self.modes_time = MY, MT
        self.gx_count, self.sa_count = gx_count, sa_count
        self.devices = gx_count * sa_count
        self.cells_x = self.slab * gx_count
        self.pairs = self.modes_y * self.modes_time
        self.own_pairs = self.pairs // self.devices
        self.rows = self.own_pairs // self.modes_time
        self.piece = self.rows * self.slab * 2
        self.group = 128 // self.modes_time
        self.groups = self.channels // self.group
        cell_count = self.cells_x * self.cells_y * self.cells_time
        self.scale_in = float(self.modes_x * self.pairs * cell_count) ** (-0.25)
        self.scale_out = float(cell_count) ** (-0.5)

    def fits(self):
        return (
            self.own_pairs == self.rows * self.modes_time
            and self.own_pairs % 16 == 0
            and self.piece % 16 == 0
            and self.modes_x == 64
            and self.channels % self.group == 0
            and self.cells_time == 128
            and self.cells_y == 128
            and inputs_fit(self)
        )


def inputs_fit(sizes):
    return sizes.sa_count == 2 and sizes.channels == 16


def spread_rows(sizes, shape, dim):
    tall = lax.broadcasted_iota(jnp.int32, shape, dim)
    short = lax.broadcasted_iota(jnp.int32, shape, 1 - dim)
    meets = tall // (2 * sizes.slab) * 2 + tall % 2 == short
    return jnp.where(meets, 1.0, 0.0).astype(jnp.bfloat16)


def forward_kernel(
    sizes, inputs, preact, cotangent, time_forward, y_forward, dz, spectra, in_rows, dz_rows, wide
):
    step = pl.program_id(0)
    slope = gelu_slope(preact[0, :, 0].astype(jnp.float32))
    gradient = (cotangent[0, :, 0].astype(jnp.float32) * slope).astype(jnp.bfloat16)
    dz[:, 0] = gradient
    first = pl.multiple_of(step * 2 * sizes.cells_y, 2 * sizes.cells_y)

    def time_rows(read, target):
        for cg in range(sizes.groups):
            left = jnp.concatenate(
                [read(cg * sizes.group + c) for c in range(sizes.group)], axis=1
            )
            both = jnp.dot(left, time_forward[...], preferred_element_type=jnp.float32)
            both = both.astype(jnp.bfloat16)
            for q in range(2):
                target[pl.ds(first + q * sizes.cells_y, sizes.cells_y), pl.ds(cg * 128, 128)] = (
                    both[:, q * 128 : (q + 1) * 128]
                )

    time_rows(lambda c: inputs[0, c, 0], in_rows)
    time_rows(lambda c: dz[c, 0], dz_rows)

    @pl.when(step == 0)
    def _():
        total = sizes.devices * sizes.piece
        tall = jnp.dot(
            spread_rows(sizes, (total, 2 * sizes.modes_y), 0), y_forward[...],
            preferred_element_type=jnp.float32,
        )
        cell = lax.broadcasted_iota(jnp.int32, tall.shape, 0) // 2 % sizes.slab
        for x in range(sizes.slab):
            wide[:, pl.ds(x * tall.shape[1], tall.shape[1])] = jnp.where(
                cell == x, tall, 0.0
            ).astype(jnp.bfloat16)

    @pl.when(step == sizes.slab - 1)
    def _():
        for field, held in enumerate((in_rows, dz_rows)):
            plane = jnp.dot(wide[...], held[...], preferred_element_type=jnp.float32)
            plane = plane.astype(jnp.bfloat16)
            for cg in range(sizes.groups):
                spectra[:, field, cg] = plane[:, cg * 128 : (cg + 1) * 128].reshape(
                    sizes.devices, sizes.piece, 128
                )


def gelu_slope(values):
    return (
        0.5 * (1.0 + lax.erf(values * root_half))
        + values * jnp.exp(-0.5 * values * values) * gauss_norm
    )


def mode_kernel(
    sizes, spectra, weight, x_input, x_grad, x_inverse, mode_grad, rows_out, hats, back
):
    step = pl.program_id(0)
    samples, groups, kt = sizes.sa_count, sizes.groups, sizes.modes_time

    @pl.when(step == 0)
    def _():
        for field, table, scale in (
            (0, x_input, sizes.scale_in),
            (1, x_grad, sizes.scale_out),
        ):
            for s in range(samples):
                for cg in range(groups):
                    block = spectra[:, s, field, cg].reshape(-1, 128)
                    summed = lax.dot_general(
                        block, table[...], (((0,), (0,)), ((), ())),
                        preferred_element_type=jnp.float32,
                    )
                    summed = (scale * summed).astype(jnp.bfloat16).astype(jnp.float32)
                    for j in range(sizes.rows):
                        for part in range(2):
                            lanes = (2 * j + part) * 128
                            for c in range(sizes.group):
                                hats[
                                    2 * field + part, s, cg * sizes.group + c, pl.ds(j * kt, kt)
                                ] = summed[c * kt : (c + 1) * kt, lanes : lanes + 128]

    low = lax.broadcasted_iota(jnp.int32, (16, 128), 1) < sizes.modes_x
    for index in range(2 * (sizes.own_pairs // 16)):
        within, block = index // (sizes.own_pairs // 16), index % (sizes.own_pairs // 16)
        channel = step * 2 + within
        cg, member = channel // sizes.group, channel % sizes.group
        rows = pl.ds(block * 16, 16)
        left = [[hats[part, s, channel, rows] for s in range(samples)] for part in range(2)]
        total = [[None, None] for _ in range(samples)]
        for o in range(sizes.channels):
            right = [[hats[2 + part, s, o, rows] for s in range(samples)] for part in range(2)]
            value = weight[within, o, rows].astype(jnp.float32)
            grad = None
            for s in range(samples):
                for part in range(2):
                    term = left[part][s] * right[part][s]
                    grad = term if grad is None else grad + term
                    term = value * right[part][s]
                    held = total[s][part]
                    total[s][part] = term if held is None else held + term
            mode_grad[within, o, rows] = grad
        j, k = divmod(block * 16, kt)
        for s in range(samples):
            real, imag = total[s]
            real = real + pltpu.roll(real, sizes.modes_x, 1)
            imag = imag + pltpu.roll(imag, sizes.modes_x, 1)
            first = pl.multiple_of(member * kt + k, 16)
            back[s, cg, pl.ds(first, 16), pl.ds(j * 128, 128)] = jnp.where(
                low, real, imag
            ).astype(jnp.bfloat16)

    @pl.when(step == sizes.channels // 2 - 1)
    def _():
        for s in range(samples):
            for cg in range(groups):
                grid_rows = lax.dot_general(
                    x_inverse[...], back[s, cg], (((1,), (1,)), ((), ())),
                    preferred_element_type=jnp.float32,
                )
                rows_out[:, s, cg] = grid_rows.astype(jnp.bfloat16).reshape(
                    sizes.gx_count, sizes.piece, 128
                )


def inverse_kernel(
    sizes, grid_rows, dz, bypass, y_inverse, time_inverse, spread, input_grad, time_rows, mixer, acc
):
    step = pl.program_id(0)
    channels, group, cells_y = sizes.channels, sizes.group, sizes.cells_y

    @pl.when(step == 0)
    def _():
        joined = jnp.concatenate(
            [grid_rows[:, cg].reshape(-1, 128) for cg in range(sizes.groups)], axis=1
        )
        total = sizes.devices * sizes.piece
        long = jnp.dot(
            y_inverse[...], spread_rows(sizes, (2 * sizes.modes_y, total), 1),
            preferred_element_type=jnp.float32,
        )
        cell = lax.broadcasted_iota(jnp.int32, long.shape, 1) // 2 % sizes.slab
        for x in range(sizes.slab):
            table = jnp.where(cell == x, long, 0.0).astype(jnp.bfloat16)
            time_rows[pl.ds(x * 2 * cells_y, 2 * cells_y)] = jnp.dot(
                table, joined, preferred_element_type=jnp.float32
            ).astype(jnp.bfloat16)
        tall = jnp.dot(spread[...], bypass[...], preferred_element_type=jnp.float32)
        wide = lax.dot_general(
            tall.astype(jnp.bfloat16), spread[...], (((1,), (1,)), ((), ())),
            preferred_element_type=jnp.float32,
        )
        row = lax.broadcasted_iota(jnp.int32, wide.shape, 0) % 16
        column = lax.broadcasted_iota(jnp.int32, wide.shape, 1) % 16
        mixer[...] = jnp.where(row == column, wide, 0.0).astype(jnp.bfloat16)

    first = pl.multiple_of(step * 2 * cells_y, 2 * cells_y)
    for cg in range(sizes.groups):
        lanes = pl.ds(cg * 128, 128)
        left = jnp.concatenate(
            [time_rows[pl.ds(first + q * cells_y, cells_y), lanes] for q in range(2)], axis=1
        )
        spectral = jnp.dot(left, time_inverse[...], preferred_element_type=jnp.float32)
        for c in range(group):
            acc[cg * group + c] = sizes.scale_in * spectral[:, c * 128 : (c + 1) * 128]
    for block in range(cells_y // 16):
        rows = pl.ds(block * 16, 16)
        mixed = jnp.dot(
            mixer[...], dz[:, 0, rows].reshape(-1, 128), preferred_element_type=jnp.float32
        ).reshape(channels, 16, 128)
        input_grad[0, :, 0, rows] = (mixed + acc[:, rows]).astype(jnp.bfloat16)


def exchange_kernel(gx_count, packet, landed, stage, near, send_sem, recv_sem, own_sem):
    place, core = lax.axis_index("gx"), lax.axis_index("sa")
    sibling = 1 - core
    mesh_ids = dict(device_id_type=pl.DeviceIdType.MESH)
    barrier = pltpu.get_barrier_semaphore()
    pl.semaphore_signal(barrier, inc=1, device_id=(place, sibling), **mesh_ids)

    @pl.loop(1, gx_count)
    def _(step):
        other = (place + step) % gx_count
        pl.semaphore_signal(barrier, inc=1, device_id=(other, core), **mesh_ids)

    pl.semaphore_wait(barrier, gx_count)
    across = pltpu.make_async_remote_copy(
        src_ref=packet.at[:, sibling], dst_ref=stage, send_sem=near.at[0], recv_sem=near.at[1],
        device_id=(place, sibling), **mesh_ids,
    )
    across.start()

    def send(which, step):
        other = (place + step) % gx_count
        source = packet.at[other, core] if which == 0 else stage.at[other]
        return pltpu.make_async_remote_copy(
            src_ref=source,
            dst_ref=landed.at[place, core if which == 0 else sibling],
            send_sem=send_sem.at[which, step],
            recv_sem=recv_sem.at[which, step],
            device_id=(other, core),
            **mesh_ids,
        )

    @pl.loop(1, gx_count)
    def _(step):
        send(0, step).start()

    own = pltpu.make_async_copy(packet.at[place, core], landed.at[place, core], own_sem.at[0])
    own.start()
    across.wait()

    @pl.loop(1, gx_count)
    def _(step):
        send(1, step).start()

    passed = pltpu.make_async_copy(stage.at[place], landed.at[place, sibling], own_sem.at[1])
    passed.start()
    own.wait()
    passed.wait()
    for which in range(2):

        @pl.loop(1, gx_count)
        def _(step):
            send(which, step).wait()


def exchange(packet, sizes, collective_id):
    return pl.pallas_call(
        functools.partial(exchange_kernel, sizes.gx_count),
        in_specs=[pl.BlockSpec(memory_space=pl.ANY)],
        out_specs=pl.BlockSpec(memory_space=pl.ANY),
        out_shape=jax.ShapeDtypeStruct(packet.shape, packet.dtype),
        scratch_shapes=[
            pltpu.VMEM((sizes.gx_count,) + packet.shape[2:], packet.dtype),
            pltpu.SemaphoreType.DMA((2,)),
            pltpu.SemaphoreType.DMA((2, sizes.gx_count)),
            pltpu.SemaphoreType.DMA((2, sizes.gx_count)),
            pltpu.SemaphoreType.DMA((2,)),
        ],
        compiler_params=pltpu.CompilerParams(
            collective_id=collective_id, has_side_effects=True, vmem_limit_bytes=VMEM_BYTES
        ),
        name="exchange",
    )(packet)


def whole(table):
    return pl.BlockSpec(table.shape, lambda *_: (0,) * table.ndim)


def shards(inputs, preact, cotangent, mode_weight, bypass_weight):
    sizes = Sizes(inputs.shape, mode_weight.shape, lax.axis_size("gx"), lax.axis_size("sa"))
    if not sizes.fits():
        return plain_shards(inputs, preact, cotangent, mode_weight, bypass_weight)
    tables_built = [jnp.asarray(table) for table in block_tables(sizes)]
    time_forward, time_inverse, y_forward, y_inverse, x_input, x_grad, x_inverse = tables_built
    channels, slab, cells_y, cells_time = inputs.shape[1:]
    params = pltpu.CompilerParams(vmem_limit_bytes=VMEM_BYTES)
    field_block = pl.BlockSpec(
        (1, channels, 1, cells_y, cells_time), lambda x: (0, 0, x, 0, 0)
    )
    dz_block = pl.BlockSpec((channels, 1, cells_y, cells_time), lambda x: (0, x, 0, 0))
    packet = (sizes.devices, 2, sizes.groups, sizes.piece, 128)
    rows_shape = (2 * slab * cells_y, sizes.groups * 128)
    dz, spectra = pl.pallas_call(
        functools.partial(forward_kernel, sizes),
        grid=(slab,),
        in_specs=[field_block] * 3 + [whole(time_forward), whole(y_forward)],
        out_specs=[dz_block, pl.BlockSpec(packet, lambda x: (0,) * 5)],
        out_shape=[
            jax.ShapeDtypeStruct(inputs.shape[1:], jnp.bfloat16),
            jax.ShapeDtypeStruct(packet, jnp.bfloat16),
        ],
        scratch_shapes=[pltpu.VMEM(rows_shape, jnp.bfloat16)] * 2
        + [pltpu.VMEM((sizes.devices * sizes.piece, rows_shape[0]), jnp.bfloat16)],
        compiler_params=params,
        name="forward",
    )(inputs, preact, cotangent, time_forward, y_forward)
    spectra = exchange(
        spectra.reshape((sizes.gx_count, sizes.sa_count) + packet[1:]), sizes, 0
    )
    own = sizes.own_pairs
    out_packet = (sizes.gx_count, sizes.sa_count, sizes.groups, sizes.piece, 128)
    mode_grad, grid_rows = pl.pallas_call(
        functools.partial(mode_kernel, sizes),
        grid=(channels // 2,),
        in_specs=[
            whole(spectra),
            pl.BlockSpec(
                (2, channels, own, 128), lambda i: (i, 0, lax.axis_index("sa"), 0)
            ),
            whole(x_input),
            whole(x_grad),
            whole(x_inverse),
        ],
        out_specs=[
            pl.BlockSpec((2, channels, own, 128), lambda i: (i, 0, 0, 0)),
            pl.BlockSpec(out_packet, lambda i: (0,) * 5),
        ],
        out_shape=[
            jax.ShapeDtypeStruct((channels, channels, own, 128), jnp.float32),
            jax.ShapeDtypeStruct(out_packet, jnp.bfloat16),
        ],
        scratch_shapes=[
            pltpu.VMEM((4, sizes.sa_count, channels, own, 128), jnp.float32),
            pltpu.VMEM((sizes.sa_count, sizes.groups, 128, sizes.rows * 128), jnp.bfloat16),
        ],
        compiler_params=params,
        name="modes",
    )(spectra, mode_weight, x_input, x_grad, x_inverse)
    grid_rows = exchange(grid_rows, sizes, 1)
    grid_rows = grid_rows.reshape((sizes.devices,) + out_packet[2:])
    spread = jnp.asarray(np.repeat(np.eye(channels), 16, axis=0).astype(jnp.bfloat16))
    input_grad = pl.pallas_call(
        functools.partial(inverse_kernel, sizes),
        grid=(slab,),
        in_specs=[
            whole(grid_rows), dz_block, whole(bypass_weight), whole(y_inverse),
            whole(time_inverse), whole(spread),
        ],
        out_specs=field_block,
        out_shape=jax.ShapeDtypeStruct(inputs.shape, jnp.bfloat16),
        scratch_shapes=[
            pltpu.VMEM(rows_shape, jnp.bfloat16),
            pltpu.VMEM((channels * 16, channels * 16), jnp.bfloat16),
            pltpu.VMEM((channels, cells_y, cells_time), jnp.float32),
        ],
        compiler_params=params,
        name="inverse",
    )(grid_rows, dz, bypass_weight, y_inverse, time_inverse, spread)
    return input_grad, mode_grad


def solution(mesh):
    placed = (
        P("sa", None, "gx", None, None),
        P("sa", None, "gx", None, None),
        P("sa", None, "gx", None, None),
        P(None, None, "gx", None),
        P(),
    )
    return jax.shard_map(
        shards,
        mesh=mesh,
        in_specs=placed,
        out_specs=(P("sa", None, "gx", None, None), P(None, None, ("gx", "sa"), None)),
        check_vma=False,
    )
```

```python
import functools
import math

import jax
import jax.numpy as jnp
import numpy as np
from jax import lax
from jax.experimental import pallas as pl
from jax.experimental.pallas import tpu as pltpu
from jax.sharding import PartitionSpec as P

MY = 64
MT = 32
VMEM_BYTES = 60 * 2**20


root_half = math.sqrt(0.5)
gauss_norm = 1.0 / math.sqrt(2.0 * math.pi)


def tables(kept_count, length, two_sided):
    frequency = jnp.arange(kept_count, dtype=jnp.int32)
    if two_sided:
        frequency = jnp.where(
            frequency < kept_count // 2, frequency, frequency + (length - kept_count)
        )
    position = jnp.arange(length, dtype=jnp.int32)
    product = frequency[:, None] * position[None, :] % length
    phase_angle = product.astype(jnp.float32) * (2.0 * math.pi / length)
    return (jnp.cos(phase_angle).astype(jnp.bfloat16), jnp.sin(phase_angle).astype(jnp.bfloat16))


def gelu_backward(preact_block, cotangent_block):
    values = preact_block.astype(jnp.float32)
    slope = (
        0.5 * (1.0 + jax.scipy.special.erf(values * root_half))
        + values * jnp.exp(-0.5 * values * values) * gauss_norm
    )
    return (cotangent_block.astype(jnp.float32) * slope).astype(jnp.bfloat16)


def gradient_term(input_hat, grad_hat, half):
    input_real = input_hat[..., :half].astype(jnp.float32)[:, None]
    input_imag = input_hat[..., half:].astype(jnp.float32)[:, None]
    grad_real = grad_hat[..., :half].astype(jnp.float32)[None]
    grad_imag = grad_hat[..., half:].astype(jnp.float32)[None]
    return jnp.concatenate(
        [
            input_real * grad_real + input_imag * grad_imag,
            input_real * grad_imag - input_imag * grad_real,
        ],
        axis=-1,
    )


def plain_shards(inputs, preact, cotangent, mode_weight, bypass_weight):
    channels = inputs.shape[1]
    slab_cells = inputs.shape[2]
    cells_y = inputs.shape[3]
    cells_time = inputs.shape[4]
    devices_x = lax.axis_size("gx")
    cells_x = slab_cells * devices_x
    modes_x = mode_weight.shape[3] // 2
    modes_y = MY
    modes_time = MT
    pair_count = modes_y * modes_time
    cell_count = cells_x * cells_y * cells_time
    scale_in = float(modes_x * pair_count * cell_count) ** (-0.25)
    scale_out = float(cell_count) ** (-0.5)
    cosine_time, sine_time = tables(modes_time, cells_time, False)
    cosine_y, sine_y = tables(modes_y, cells_y, True)
    cosine_x, sine_x = tables(modes_x, cells_x, True)
    forward_time = jnp.concatenate([cosine_time.T, -sine_time.T], axis=1)
    inverse_time = jnp.concatenate([cosine_time, -sine_time], axis=0)
    plane_table = jnp.stack([jnp.stack([cosine_y, sine_y], -1), jnp.stack([-sine_y, cosine_y], -1)])
    x_forward = jnp.stack(
        [jnp.concatenate([cosine_x, -sine_x], 0).T, jnp.concatenate([sine_x, cosine_x], 0).T], 1
    )
    x_inverse = jnp.stack(
        [jnp.concatenate([cosine_x, -sine_x], 0), jnp.concatenate([sine_x, cosine_x], 0)], -1
    )

    def spectra(field):
        sectioned = jnp.dot(
            field.reshape(-1, cells_time), forward_time, preferred_element_type=jnp.float32
        ).astype(jnp.bfloat16)
        sectioned = sectioned.reshape(channels, slab_cells, cells_y, 2, modes_time)
        plane = jnp.einsum(
            "cxyqk,ajyq->jkcxa", sectioned, plane_table, preferred_element_type=jnp.float32
        ).astype(jnp.bfloat16)
        return plane.reshape(pair_count, channels, slab_cells, 2)

    def x_transform(block, factor):
        summed = jnp.einsum("pcxq,xqr->cpr", block, x_forward, preferred_element_type=jnp.float32)
        return (factor * summed).astype(jnp.bfloat16)

    dz_field = gelu_backward(preact[0], cotangent[0])
    input_hat = x_transform(
        lax.all_to_all(spectra(inputs[0]), "gx", split_axis=0, concat_axis=2, tiled=True), scale_in
    )
    grad_hat = x_transform(
        lax.all_to_all(spectra(dz_field), "gx", split_axis=0, concat_axis=2, tiled=True), scale_out
    )
    mode_grad = lax.psum_scatter(
        gradient_term(input_hat, grad_hat, modes_x).astype(jnp.bfloat16),
        "sa",
        scatter_dimension=2,
        tiled=True,
    ).astype(jnp.float32)
    weights = mode_weight.astype(jnp.float32)
    grad_real = grad_hat[..., :modes_x].astype(jnp.float32)[None]
    grad_imag = grad_hat[..., modes_x:].astype(jnp.float32)[None]
    weight_real = weights[..., :modes_x]
    weight_imag = weights[..., modes_x:]
    back_real = jnp.sum(weight_real * grad_real + weight_imag * grad_imag, axis=1)
    back_imag = jnp.sum(weight_real * grad_imag - weight_imag * grad_real, axis=1)
    back_hat = jnp.concatenate([back_real, back_imag], axis=-1).astype(jnp.bfloat16)
    grid_rows = jnp.einsum(
        "cpr,rxq->pcxq", back_hat, x_inverse, preferred_element_type=jnp.float32
    ).astype(jnp.bfloat16)
    block = lax.all_to_all(grid_rows, "gx", split_axis=2, concat_axis=0, tiled=True)
    items = block.shape[1]
    plane = block.reshape(modes_y, modes_time, items, slab_cells, 2)
    joined = jnp.einsum(
        "jkcxa,ajyq->cxyqk", plane, plane_table, preferred_element_type=jnp.float32
    ).astype(jnp.bfloat16)
    spectral = jnp.dot(
        joined.reshape(-1, 2 * modes_time), inverse_time, preferred_element_type=jnp.float32
    )
    spectral_grad = scale_in * spectral.reshape(items, slab_cells, cells_y, cells_time)
    bypass = jnp.dot(
        bypass_weight, dz_field.reshape(channels, -1), preferred_element_type=jnp.float32
    ).reshape(dz_field.shape)
    input_grad = (spectral_grad + bypass).astype(jnp.bfloat16)[None]
    return (input_grad, mode_grad)


def host_tables(kept_count, length, two_sided):
    frequency = np.arange(kept_count)
    if two_sided:
        frequency = np.where(
            frequency < kept_count // 2, frequency, frequency + (length - kept_count)
        )
    product = frequency[:, None] * np.arange(length)[None, :] % length
    angle = product.astype(np.float32) * np.float32(2.0 * math.pi / length)
    return np.cos(angle).astype(np.float32), np.sin(angle).astype(np.float32)


def block_tables(sizes):
    ct, st = host_tables(sizes.modes_time, sizes.cells_time, False)
    cy, sy = host_tables(sizes.modes_y, sizes.cells_y, True)
    cx, sx = host_tables(sizes.modes_x, sizes.cells_x, True)
    group = np.eye(sizes.group, dtype=np.float32)
    rows = np.eye(sizes.rows, dtype=np.float32)
    time = np.stack([ct, -st])
    time_forward = np.einsum("cd,qkt->ctqdk", group, time)
    time_forward = time_forward.reshape(sizes.group * sizes.cells_time, -1)
    time_inverse = time_forward.T
    plane = np.stack([np.stack([cy, sy]), np.stack([-sy, cy])])
    plane = plane.reshape(2, 2, sizes.devices, sizes.rows, sizes.cells_y)
    plane = np.einsum("qpdjy->djqpy", plane)
    y_forward = plane.reshape(2 * sizes.modes_y, -1)
    y_inverse = y_forward.T
    x_table = np.stack(
        [np.concatenate([cx, -sx], 0).T, np.concatenate([sx, cx], 0).T], 1
    )
    x_table = x_table.reshape(-1, sizes.slab, 2, 2 * sizes.modes_x)
    real, imag = x_table[..., : sizes.modes_x], x_table[..., sizes.modes_x :]

    def x_rows(table):
        wide = np.einsum("gxqr,jl->gjxqlr", table, rows)
        return wide.reshape(-1, sizes.rows * table.shape[-1])

    x_input = x_rows(np.concatenate([real, real, imag, imag], -1))
    x_grad = x_rows(np.concatenate([real, imag, imag, -real], -1))
    x_inverse = x_rows(x_table)
    everything = (time_forward, time_inverse, y_forward, y_inverse, x_input, x_grad, x_inverse)
    return [table.astype(jnp.bfloat16) for table in everything]


class Sizes:
    def __init__(self, inputs, mode_weight, gx_count, sa_count):
        _, self.channels, self.slab, self.cells_y, self.cells_time = inputs
        self.modes_x = mode_weight[3] // 2
        self.modes_y, self.modes_time = MY, MT
        self.gx_count, self.sa_count = gx_count, sa_count
        self.devices = gx_count * sa_count
        self.cells_x = self.slab * gx_count
        self.pairs = self.modes_y * self.modes_time
        self.own_pairs = self.pairs // self.devices
        self.rows = self.own_pairs // self.modes_time
        self.piece = self.rows * self.slab * 2
        self.group = 128 // self.modes_time
        self.groups = self.channels // self.group
        cell_count = self.cells_x * self.cells_y * self.cells_time
        self.scale_in = float(self.modes_x * self.pairs * cell_count) ** (-0.25)
        self.scale_out = float(cell_count) ** (-0.5)

    def fits(self):
        return (
            self.own_pairs == self.rows * self.modes_time
            and self.own_pairs % 16 == 0
            and self.piece % 16 == 0
            and self.modes_x == 64
            and self.channels % self.group == 0
            and self.cells_time == 128
            and self.cells_y == 128
            and inputs_fit(self)
        )


def inputs_fit(sizes):
    return sizes.sa_count == 2 and sizes.channels == 16


def spread_rows(sizes, shape, dim):
    tall = lax.broadcasted_iota(jnp.int32, shape, dim)
    short = lax.broadcasted_iota(jnp.int32, shape, 1 - dim)
    meets = tall // (2 * sizes.slab) * 2 + tall % 2 == short
    return jnp.where(meets, 1.0, 0.0).astype(jnp.bfloat16)


def forward_kernel(
    sizes, inputs, preact, cotangent, time_forward, y_forward, dz, spectra, in_rows, dz_rows, wide
):
    step = pl.program_id(0)
    slope = gelu_slope(preact[0, :, 0].astype(jnp.float32))
    gradient = (cotangent[0, :, 0].astype(jnp.float32) * slope).astype(jnp.bfloat16)
    dz[:, 0] = gradient
    first = pl.multiple_of(step * 2 * sizes.cells_y, 2 * sizes.cells_y)

    def time_rows(read, target):
        for cg in range(sizes.groups):
            left = jnp.concatenate(
                [read(cg * sizes.group + c) for c in range(sizes.group)], axis=1
            )
            both = jnp.dot(left, time_forward[...], preferred_element_type=jnp.float32)
            both = both.astype(jnp.bfloat16)
            for q in range(2):
                target[pl.ds(first + q * sizes.cells_y, sizes.cells_y), pl.ds(cg * 128, 128)] = (
                    both[:, q * 128 : (q + 1) * 128]
                )

    time_rows(lambda c: inputs[0, c, 0], in_rows)
    time_rows(lambda c: dz[c, 0], dz_rows)

    @pl.when(step == 0)
    def _():
        total = sizes.devices * sizes.piece
        tall = jnp.dot(
            spread_rows(sizes, (total, 2 * sizes.modes_y), 0), y_forward[...],
            preferred_element_type=jnp.float32,
        )
        cell = lax.broadcasted_iota(jnp.int32, tall.shape, 0) // 2 % sizes.slab
        for x in range(sizes.slab):
            wide[:, pl.ds(x * tall.shape[1], tall.shape[1])] = jnp.where(
                cell == x, tall, 0.0
            ).astype(jnp.bfloat16)

    @pl.when(step == sizes.slab - 1)
    def _():
        for field, held in enumerate((in_rows, dz_rows)):
            plane = jnp.dot(wide[...], held[...], preferred_element_type=jnp.float32)
            plane = plane.astype(jnp.bfloat16)
            for cg in range(sizes.groups):
                spectra[:, field, cg] = plane[:, cg * 128 : (cg + 1) * 128].reshape(
                    sizes.devices, sizes.piece, 128
                )


def gelu_slope(values):
    return (
        0.5 * (1.0 + lax.erf(values * root_half))
        + values * jnp.exp(-0.5 * values * values) * gauss_norm
    )


def mode_kernel(
    sizes, spectra, weight, x_input, x_grad, x_inverse, mode_grad, rows_out, hats, back
):
    step = pl.program_id(0)
    samples, groups, kt = sizes.sa_count, sizes.groups, sizes.modes_time

    @pl.when(step == 0)
    def _():
        for field, table, scale in (
            (0, x_input, sizes.scale_in),
            (1, x_grad, sizes.scale_out),
        ):
            for s in range(samples):
                for cg in range(groups):
                    block = spectra[:, s, field, cg].reshape(-1, 128)
                    summed = lax.dot_general(
                        block, table[...], (((0,), (0,)), ((), ())),
                        preferred_element_type=jnp.float32,
                    )
                    summed = (scale * summed).astype(jnp.bfloat16).astype(jnp.float32)
                    for j in range(sizes.rows):
                        for part in range(2):
                            lanes = (2 * j + part) * 128
                            for c in range(sizes.group):
                                hats[
                                    2 * field + part, s, cg * sizes.group + c, pl.ds(j * kt, kt)
                                ] = summed[c * kt : (c + 1) * kt, lanes : lanes + 128]

    low = lax.broadcasted_iota(jnp.int32, (16, 128), 1) < sizes.modes_x
    for index in range(2 * (sizes.own_pairs // 16)):
        within, block = index // (sizes.own_pairs // 16), index % (sizes.own_pairs // 16)
        channel = step * 2 + within
        cg, member = channel // sizes.group, channel % sizes.group
        rows = pl.ds(block * 16, 16)
        left = [[hats[part, s, channel, rows] for s in range(samples)] for part in range(2)]
        total = [[None, None] for _ in range(samples)]
        for o in range(sizes.channels):
            right = [[hats[2 + part, s, o, rows] for s in range(samples)] for part in range(2)]
            value = weight[within, o, rows].astype(jnp.float32)
            grad = None
            for s in range(samples):
                for part in range(2):
                    term = left[part][s] * right[part][s]
                    grad = term if grad is None else grad + term
                    term = value * right[part][s]
                    held = total[s][part]
                    total[s][part] = term if held is None else held + term
            mode_grad[within, o, rows] = grad
        j, k = divmod(block * 16, kt)
        for s in range(samples):
            real, imag = total[s]
            real = real + pltpu.roll(real, sizes.modes_x, 1)
            imag = imag + pltpu.roll(imag, sizes.modes_x, 1)
            first = pl.multiple_of(member * kt + k, 16)
            back[s, cg, pl.ds(first, 16), pl.ds(j * 128, 128)] = jnp.where(
                low, real, imag
            ).astype(jnp.bfloat16)

    @pl.when(step == sizes.channels // 2 - 1)
    def _():
        for s in range(samples):
            for cg in range(groups):
                grid_rows = lax.dot_general(
                    x_inverse[...], back[s, cg], (((1,), (1,)), ((), ())),
                    preferred_element_type=jnp.float32,
                )
                rows_out[:, s, cg] = grid_rows.astype(jnp.bfloat16).reshape(
                    sizes.gx_count, sizes.piece, 128
                )


def inverse_kernel(
    sizes, grid_rows, dz, bypass, y_inverse, time_inverse, spread, input_grad, time_rows, mixer, acc
):
    step = pl.program_id(0)
    channels, group, cells_y = sizes.channels, sizes.group, sizes.cells_y

    @pl.when(step == 0)
    def _():
        joined = jnp.concatenate(
            [grid_rows[:, cg].reshape(-1, 128) for cg in range(sizes.groups)], axis=1
        )
        total = sizes.devices * sizes.piece
        long = jnp.dot(
            y_inverse[...], spread_rows(sizes, (2 * sizes.modes_y, total), 1),
            preferred_element_type=jnp.float32,
        )
        cell = lax.broadcasted_iota(jnp.int32, long.shape, 1) // 2 % sizes.slab
        for x in range(sizes.slab):
            table = jnp.where(cell == x, long, 0.0).astype(jnp.bfloat16)
            time_rows[pl.ds(x * 2 * cells_y, 2 * cells_y)] = jnp.dot(
                table, joined, preferred_element_type=jnp.float32
            ).astype(jnp.bfloat16)
        tall = jnp.dot(spread[...], bypass[...], preferred_element_type=jnp.float32)
        wide = lax.dot_general(
            tall.astype(jnp.bfloat16), spread[...], (((1,), (1,)), ((), ())),
            preferred_element_type=jnp.float32,
        )
        row = lax.broadcasted_iota(jnp.int32, wide.shape, 0) % 16
        column = lax.broadcasted_iota(jnp.int32, wide.shape, 1) % 16
        mixer[...] = jnp.where(row == column, wide, 0.0).astype(jnp.bfloat16)

    first = pl.multiple_of(step * 2 * cells_y, 2 * cells_y)
    for cg in range(sizes.groups):
        lanes = pl.ds(cg * 128, 128)
        left = jnp.concatenate(
            [time_rows[pl.ds(first + q * cells_y, cells_y), lanes] for q in range(2)], axis=1
        )
        spectral = jnp.dot(left, time_inverse[...], preferred_element_type=jnp.float32)
        for c in range(group):
            acc[cg * group + c] = sizes.scale_in * spectral[:, c * 128 : (c + 1) * 128]
    for block in range(cells_y // 16):
        rows = pl.ds(block * 16, 16)
        mixed = jnp.dot(
            mixer[...], dz[:, 0, rows].reshape(-1, 128), preferred_element_type=jnp.float32
        ).reshape(channels, 16, 128)
        input_grad[0, :, 0, rows] = (mixed + acc[:, rows]).astype(jnp.bfloat16)


def sibling_kernel(packet, landed, near, own_sem):
    place, core = lax.axis_index("gx"), lax.axis_index("sa")
    sibling = 1 - core
    own = pltpu.make_async_copy(packet.at[:, core], landed.at[:, core], own_sem)
    own.start()
    mesh_ids = dict(device_id=(place, sibling), device_id_type=pl.DeviceIdType.MESH)
    barrier = pltpu.get_barrier_semaphore()
    pl.semaphore_signal(barrier, inc=1, **mesh_ids)
    pl.semaphore_wait(barrier, 1)
    across = pltpu.make_async_remote_copy(
        src_ref=packet.at[:, sibling], dst_ref=landed.at[:, core],
        send_sem=near.at[0], recv_sem=near.at[1], **mesh_ids,
    )
    across.start()
    own.wait()
    across.wait()


def exchange(packet, collective_id):
    swapped = pl.pallas_call(
        sibling_kernel,
        in_specs=[pl.BlockSpec(memory_space=pl.ANY)],
        out_specs=pl.BlockSpec(memory_space=pl.ANY),
        out_shape=jax.ShapeDtypeStruct(packet.shape, packet.dtype),
        scratch_shapes=[pltpu.SemaphoreType.DMA((2,)), pltpu.SemaphoreType.DMA(())],
        compiler_params=pltpu.CompilerParams(
            collective_id=collective_id, has_side_effects=True, vmem_limit_bytes=VMEM_BYTES
        ),
        name="sibling",
    )(packet)
    return lax.all_to_all(swapped, "gx", split_axis=0, concat_axis=0, tiled=True)


def whole(table):
    return pl.BlockSpec(table.shape, lambda *_: (0,) * table.ndim)


def shards(inputs, preact, cotangent, mode_weight, bypass_weight):
    sizes = Sizes(inputs.shape, mode_weight.shape, lax.axis_size("gx"), lax.axis_size("sa"))
    if not sizes.fits():
        return plain_shards(inputs, preact, cotangent, mode_weight, bypass_weight)
    tables_built = [jnp.asarray(table) for table in block_tables(sizes)]
    time_forward, time_inverse, y_forward, y_inverse, x_input, x_grad, x_inverse = tables_built
    channels, slab, cells_y, cells_time = inputs.shape[1:]
    params = pltpu.CompilerParams(vmem_limit_bytes=VMEM_BYTES)
    field_block = pl.BlockSpec(
        (1, channels, 1, cells_y, cells_time), lambda x: (0, 0, x, 0, 0)
    )
    dz_block = pl.BlockSpec((channels, 1, cells_y, cells_time), lambda x: (0, x, 0, 0))
    packet = (sizes.devices, 2, sizes.groups, sizes.piece, 128)
    rows_shape = (2 * slab * cells_y, sizes.groups * 128)
    dz, spectra = pl.pallas_call(
        functools.partial(forward_kernel, sizes),
        grid=(slab,),
        in_specs=[field_block] * 3 + [whole(time_forward), whole(y_forward)],
        out_specs=[dz_block, pl.BlockSpec(packet, lambda x: (0,) * 5)],
        out_shape=[
            jax.ShapeDtypeStruct(inputs.shape[1:], jnp.bfloat16),
            jax.ShapeDtypeStruct(packet, jnp.bfloat16),
        ],
        scratch_shapes=[pltpu.VMEM(rows_shape, jnp.bfloat16)] * 2
        + [pltpu.VMEM((sizes.devices * sizes.piece, rows_shape[0]), jnp.bfloat16)],
        compiler_params=params,
        name="forward",
    )(inputs, preact, cotangent, time_forward, y_forward)
    spectra = exchange(spectra.reshape((sizes.gx_count, sizes.sa_count) + packet[1:]), 0)
    own = sizes.own_pairs
    out_packet = (sizes.gx_count, sizes.sa_count, sizes.groups, sizes.piece, 128)
    mode_grad, grid_rows = pl.pallas_call(
        functools.partial(mode_kernel, sizes),
        grid=(channels // 2,),
        in_specs=[
            whole(spectra),
            pl.BlockSpec(
                (2, channels, own, 128), lambda i: (i, 0, lax.axis_index("sa"), 0)
            ),
            whole(x_input),
            whole(x_grad),
            whole(x_inverse),
        ],
        out_specs=[
            pl.BlockSpec((2, channels, own, 128), lambda i: (i, 0, 0, 0)),
            pl.BlockSpec(out_packet, lambda i: (0,) * 5),
        ],
        out_shape=[
            jax.ShapeDtypeStruct((channels, channels, own, 128), jnp.float32),
            jax.ShapeDtypeStruct(out_packet, jnp.bfloat16),
        ],
        scratch_shapes=[
            pltpu.VMEM((4, sizes.sa_count, channels, own, 128), jnp.float32),
            pltpu.VMEM((sizes.sa_count, sizes.groups, 128, sizes.rows * 128), jnp.bfloat16),
        ],
        compiler_params=params,
        name="modes",
    )(spectra, mode_weight, x_input, x_grad, x_inverse)
    grid_rows = exchange(grid_rows, 1)
    grid_rows = grid_rows.reshape((sizes.devices,) + out_packet[2:])
    spread = jnp.asarray(np.repeat(np.eye(channels), 16, axis=0).astype(jnp.bfloat16))
    input_grad = pl.pallas_call(
        functools.partial(inverse_kernel, sizes),
        grid=(slab,),
        in_specs=[
            whole(grid_rows), dz_block, whole(bypass_weight), whole(y_inverse),
            whole(time_inverse), whole(spread),
        ],
        out_specs=field_block,
        out_shape=jax.ShapeDtypeStruct(inputs.shape, jnp.bfloat16),
        scratch_shapes=[
            pltpu.VMEM(rows_shape, jnp.bfloat16),
            pltpu.VMEM((channels * 16, channels * 16), jnp.bfloat16),
            pltpu.VMEM((channels, cells_y, cells_time), jnp.float32),
        ],
        compiler_params=params,
        name="inverse",
    )(grid_rows, dz, bypass_weight, y_inverse, time_inverse, spread)
    return input_grad, mode_grad


def solution(mesh):
    placed = (
        P("sa", None, "gx", None, None),
        P("sa", None, "gx", None, None),
        P("sa", None, "gx", None, None),
        P(None, None, "gx", None),
        P(),
    )
    return jax.shard_map(
        shards,
        mesh=mesh,
        in_specs=placed,
        out_specs=(P("sa", None, "gx", None, None), P(None, None, ("gx", "sa"), None)),
        check_vma=False,
    )
```

```python
import functools
import math

import jax
import jax.numpy as jnp
import numpy as np
from jax import lax
from jax.experimental import pallas as pl
from jax.experimental.pallas import tpu as pltpu
from jax.sharding import PartitionSpec as P

MY = 64
MT = 32
VMEM_BYTES = 60 * 2**20


root_half = math.sqrt(0.5)
gauss_norm = 1.0 / math.sqrt(2.0 * math.pi)


def tables(kept_count, length, two_sided):
    frequency = jnp.arange(kept_count, dtype=jnp.int32)
    if two_sided:
        frequency = jnp.where(
            frequency < kept_count // 2, frequency, frequency + (length - kept_count)
        )
    position = jnp.arange(length, dtype=jnp.int32)
    product = frequency[:, None] * position[None, :] % length
    phase_angle = product.astype(jnp.float32) * (2.0 * math.pi / length)
    return (jnp.cos(phase_angle).astype(jnp.bfloat16), jnp.sin(phase_angle).astype(jnp.bfloat16))


def gelu_backward(preact_block, cotangent_block):
    values = preact_block.astype(jnp.float32)
    slope = (
        0.5 * (1.0 + jax.scipy.special.erf(values * root_half))
        + values * jnp.exp(-0.5 * values * values) * gauss_norm
    )
    return (cotangent_block.astype(jnp.float32) * slope).astype(jnp.bfloat16)


def gradient_term(input_hat, grad_hat, half):
    input_real = input_hat[..., :half].astype(jnp.float32)[:, None]
    input_imag = input_hat[..., half:].astype(jnp.float32)[:, None]
    grad_real = grad_hat[..., :half].astype(jnp.float32)[None]
    grad_imag = grad_hat[..., half:].astype(jnp.float32)[None]
    return jnp.concatenate(
        [
            input_real * grad_real + input_imag * grad_imag,
            input_real * grad_imag - input_imag * grad_real,
        ],
        axis=-1,
    )


def plain_shards(inputs, preact, cotangent, mode_weight, bypass_weight):
    channels = inputs.shape[1]
    slab_cells = inputs.shape[2]
    cells_y = inputs.shape[3]
    cells_time = inputs.shape[4]
    devices_x = lax.axis_size("gx")
    cells_x = slab_cells * devices_x
    modes_x = mode_weight.shape[3] // 2
    modes_y = MY
    modes_time = MT
    pair_count = modes_y * modes_time
    cell_count = cells_x * cells_y * cells_time
    scale_in = float(modes_x * pair_count * cell_count) ** (-0.25)
    scale_out = float(cell_count) ** (-0.5)
    cosine_time, sine_time = tables(modes_time, cells_time, False)
    cosine_y, sine_y = tables(modes_y, cells_y, True)
    cosine_x, sine_x = tables(modes_x, cells_x, True)
    forward_time = jnp.concatenate([cosine_time.T, -sine_time.T], axis=1)
    inverse_time = jnp.concatenate([cosine_time, -sine_time], axis=0)
    plane_table = jnp.stack([jnp.stack([cosine_y, sine_y], -1), jnp.stack([-sine_y, cosine_y], -1)])
    x_forward = jnp.stack(
        [jnp.concatenate([cosine_x, -sine_x], 0).T, jnp.concatenate([sine_x, cosine_x], 0).T], 1
    )
    x_inverse = jnp.stack(
        [jnp.concatenate([cosine_x, -sine_x], 0), jnp.concatenate([sine_x, cosine_x], 0)], -1
    )

    def spectra(field):
        sectioned = jnp.dot(
            field.reshape(-1, cells_time), forward_time, preferred_element_type=jnp.float32
        ).astype(jnp.bfloat16)
        sectioned = sectioned.reshape(channels, slab_cells, cells_y, 2, modes_time)
        plane = jnp.einsum(
            "cxyqk,ajyq->jkcxa", sectioned, plane_table, preferred_element_type=jnp.float32
        ).astype(jnp.bfloat16)
        return plane.reshape(pair_count, channels, slab_cells, 2)

    def x_transform(block, factor):
        summed = jnp.einsum("pcxq,xqr->cpr", block, x_forward, preferred_element_type=jnp.float32)
        return (factor * summed).astype(jnp.bfloat16)

    dz_field = gelu_backward(preact[0], cotangent[0])
    input_hat = x_transform(
        lax.all_to_all(spectra(inputs[0]), "gx", split_axis=0, concat_axis=2, tiled=True), scale_in
    )
    grad_hat = x_transform(
        lax.all_to_all(spectra(dz_field), "gx", split_axis=0, concat_axis=2, tiled=True), scale_out
    )
    mode_grad = lax.psum_scatter(
        gradient_term(input_hat, grad_hat, modes_x).astype(jnp.bfloat16),
        "sa",
        scatter_dimension=2,
        tiled=True,
    ).astype(jnp.float32)
    weights = mode_weight.astype(jnp.float32)
    grad_real = grad_hat[..., :modes_x].astype(jnp.float32)[None]
    grad_imag = grad_hat[..., modes_x:].astype(jnp.float32)[None]
    weight_real = weights[..., :modes_x]
    weight_imag = weights[..., modes_x:]
    back_real = jnp.sum(weight_real * grad_real + weight_imag * grad_imag, axis=1)
    back_imag = jnp.sum(weight_real * grad_imag - weight_imag * grad_real, axis=1)
    back_hat = jnp.concatenate([back_real, back_imag], axis=-1).astype(jnp.bfloat16)
    grid_rows = jnp.einsum(
        "cpr,rxq->pcxq", back_hat, x_inverse, preferred_element_type=jnp.float32
    ).astype(jnp.bfloat16)
    block = lax.all_to_all(grid_rows, "gx", split_axis=2, concat_axis=0, tiled=True)
    items = block.shape[1]
    plane = block.reshape(modes_y, modes_time, items, slab_cells, 2)
    joined = jnp.einsum(
        "jkcxa,ajyq->cxyqk", plane, plane_table, preferred_element_type=jnp.float32
    ).astype(jnp.bfloat16)
    spectral = jnp.dot(
        joined.reshape(-1, 2 * modes_time), inverse_time, preferred_element_type=jnp.float32
    )
    spectral_grad = scale_in * spectral.reshape(items, slab_cells, cells_y, cells_time)
    bypass = jnp.dot(
        bypass_weight, dz_field.reshape(channels, -1), preferred_element_type=jnp.float32
    ).reshape(dz_field.shape)
    input_grad = (spectral_grad + bypass).astype(jnp.bfloat16)[None]
    return (input_grad, mode_grad)


def host_tables(kept_count, length, two_sided):
    frequency = np.arange(kept_count)
    if two_sided:
        frequency = np.where(
            frequency < kept_count // 2, frequency, frequency + (length - kept_count)
        )
    product = frequency[:, None] * np.arange(length)[None, :] % length
    angle = product.astype(np.float32) * np.float32(2.0 * math.pi / length)
    return np.cos(angle).astype(np.float32), np.sin(angle).astype(np.float32)


def block_tables(sizes):
    ct, st = host_tables(sizes.modes_time, sizes.cells_time, False)
    cy, sy = host_tables(sizes.modes_y, sizes.cells_y, True)
    cx, sx = host_tables(sizes.modes_x, sizes.cells_x, True)
    group = np.eye(sizes.group, dtype=np.float32)
    rows = np.eye(sizes.rows, dtype=np.float32)
    time = np.stack([ct, -st])
    time_forward = np.einsum("cd,qkt->ctqdk", group, time)
    time_forward = time_forward.reshape(sizes.group * sizes.cells_time, -1)
    time_inverse = time_forward.T
    plane = np.stack([np.stack([cy, sy]), np.stack([-sy, cy])])
    plane = plane.reshape(2, 2, sizes.devices, sizes.rows, sizes.cells_y)
    plane = np.einsum("qpdjy->djqpy", plane)
    y_forward = plane.reshape(2 * sizes.modes_y, -1)
    y_inverse = y_forward.T
    x_table = np.stack(
        [np.concatenate([cx, -sx], 0).T, np.concatenate([sx, cx], 0).T], 1
    )
    x_table = x_table.reshape(-1, sizes.slab, 2, 2 * sizes.modes_x)
    real, imag = x_table[..., : sizes.modes_x], x_table[..., sizes.modes_x :]

    def x_rows(table):
        wide = np.einsum("gxqr,jl->gjxqlr", table, rows)
        return wide.reshape(-1, sizes.rows * table.shape[-1])

    x_input = x_rows(np.concatenate([real, real, imag, imag], -1))
    x_grad = x_rows(np.concatenate([real, imag, imag, -real], -1))
    x_inverse = x_rows(x_table)
    everything = (time_forward, time_inverse, y_forward, y_inverse, x_input, x_grad, x_inverse)
    return [table.astype(jnp.bfloat16) for table in everything]


class Sizes:
    def __init__(self, inputs, mode_weight, gx_count, sa_count):
        _, self.channels, self.slab, self.cells_y, self.cells_time = inputs
        self.modes_x = mode_weight[3] // 2
        self.modes_y, self.modes_time = MY, MT
        self.gx_count, self.sa_count = gx_count, sa_count
        self.devices = gx_count * sa_count
        self.cells_x = self.slab * gx_count
        self.pairs = self.modes_y * self.modes_time
        self.own_pairs = self.pairs // self.devices
        self.rows = self.own_pairs // self.modes_time
        self.piece = self.rows * self.slab * 2
        self.group = 128 // self.modes_time
        self.groups = self.channels // self.group
        cell_count = self.cells_x * self.cells_y * self.cells_time
        self.scale_in = float(self.modes_x * self.pairs * cell_count) ** (-0.25)
        self.scale_out = float(cell_count) ** (-0.5)

    def fits(self):
        return (
            self.own_pairs == self.rows * self.modes_time
            and self.own_pairs % 16 == 0
            and self.piece % 16 == 0
            and self.modes_x == 64
            and self.channels % self.group == 0
            and self.cells_time == 128
            and self.cells_y == 128
            and inputs_fit(self)
        )


def inputs_fit(sizes):
    return sizes.sa_count == 2 and sizes.channels == 16


def spread_rows(sizes, shape, dim):
    tall = lax.broadcasted_iota(jnp.int32, shape, dim)
    short = lax.broadcasted_iota(jnp.int32, shape, 1 - dim)
    meets = tall // (2 * sizes.slab) * 2 + tall % 2 == short
    return jnp.where(meets, 1.0, 0.0).astype(jnp.bfloat16)


def forward_kernel(
    sizes, inputs, preact, cotangent, time_forward, y_forward, dz, spectra, in_rows, dz_rows, wide
):
    step = pl.program_id(0)
    slope = gelu_slope(preact[0, :, 0].astype(jnp.float32))
    gradient = (cotangent[0, :, 0].astype(jnp.float32) * slope).astype(jnp.bfloat16)
    dz[:, 0] = gradient
    first = pl.multiple_of(step * 2 * sizes.cells_y, 2 * sizes.cells_y)

    def time_rows(read, target):
        for cg in range(sizes.groups):
            left = jnp.concatenate(
                [read(cg * sizes.group + c) for c in range(sizes.group)], axis=1
            )
            both = jnp.dot(left, time_forward[...], preferred_element_type=jnp.float32)
            both = both.astype(jnp.bfloat16)
            for q in range(2):
                target[pl.ds(first + q * sizes.cells_y, sizes.cells_y), pl.ds(cg * 128, 128)] = (
                    both[:, q * 128 : (q + 1) * 128]
                )

    time_rows(lambda c: inputs[0, c, 0], in_rows)
    time_rows(lambda c: dz[c, 0], dz_rows)

    @pl.when(step == 0)
    def _():
        total = sizes.devices * sizes.piece
        tall = jnp.dot(
            spread_rows(sizes, (total, 2 * sizes.modes_y), 0), y_forward[...],
            preferred_element_type=jnp.float32,
        )
        cell = lax.broadcasted_iota(jnp.int32, tall.shape, 0) // 2 % sizes.slab
        for x in range(sizes.slab):
            wide[:, pl.ds(x * tall.shape[1], tall.shape[1])] = jnp.where(
                cell == x, tall, 0.0
            ).astype(jnp.bfloat16)

    @pl.when(step == sizes.slab - 1)
    def _():
        for field, held in enumerate((in_rows, dz_rows)):
            plane = jnp.dot(wide[...], held[...], preferred_element_type=jnp.float32)
            plane = plane.astype(jnp.bfloat16)
            for cg in range(sizes.groups):
                rows = pl.ds((field * sizes.groups + cg) * sizes.piece, sizes.piece)
                spectra[:, rows] = plane[:, cg * 128 : (cg + 1) * 128].reshape(
                    sizes.devices, sizes.piece, 128
                )


def gelu_slope(values):
    return (
        0.5 * (1.0 + lax.erf(values * root_half))
        + values * jnp.exp(-0.5 * values * values) * gauss_norm
    )


def mode_kernel(
    sizes, spectra, weight, x_input, x_grad, x_inverse, mode_grad, rows_out, hats, back
):
    step = pl.program_id(0)
    samples, groups, kt = sizes.sa_count, sizes.groups, sizes.modes_time

    @pl.when(step == 0)
    def _():
        for field, table, scale in (
            (0, x_input, sizes.scale_in),
            (1, x_grad, sizes.scale_out),
        ):
            for s in range(samples):
                for cg in range(groups):
                    first = (field * groups + cg) * sizes.piece
                    block = spectra[:, s, pl.ds(first, sizes.piece)].reshape(-1, 128)
                    summed = lax.dot_general(
                        block, table[...], (((0,), (0,)), ((), ())),
                        preferred_element_type=jnp.float32,
                    )
                    summed = (scale * summed).astype(jnp.bfloat16).astype(jnp.float32)
                    for j in range(sizes.rows):
                        for part in range(2):
                            lanes = (2 * j + part) * 128
                            for c in range(sizes.group):
                                hats[
                                    2 * field + part, s, cg * sizes.group + c, pl.ds(j * kt, kt)
                                ] = summed[c * kt : (c + 1) * kt, lanes : lanes + 128]

    low = lax.broadcasted_iota(jnp.int32, (16, 128), 1) < sizes.modes_x
    for index in range(2 * (sizes.own_pairs // 16)):
        within, block = index // (sizes.own_pairs // 16), index % (sizes.own_pairs // 16)
        channel = step * 2 + within
        cg, member = channel // sizes.group, channel % sizes.group
        rows = pl.ds(block * 16, 16)
        left = [[hats[part, s, channel, rows] for s in range(samples)] for part in range(2)]
        total = [[None, None] for _ in range(samples)]
        for o in range(sizes.channels):
            right = [[hats[2 + part, s, o, rows] for s in range(samples)] for part in range(2)]
            value = weight[within, o, rows].astype(jnp.float32)
            grad = None
            for s in range(samples):
                for part in range(2):
                    term = left[part][s] * right[part][s]
                    grad = term if grad is None else grad + term
                    term = value * right[part][s]
                    held = total[s][part]
                    total[s][part] = term if held is None else held + term
            mode_grad[within, o, rows] = grad
        j, k = divmod(block * 16, kt)
        for s in range(samples):
            real, imag = total[s]
            real = real + pltpu.roll(real, sizes.modes_x, 1)
            imag = imag + pltpu.roll(imag, sizes.modes_x, 1)
            first = pl.multiple_of(member * kt + k, 16)
            back[s, cg, pl.ds(first, 16), pl.ds(j * 128, 128)] = jnp.where(
                low, real, imag
            ).astype(jnp.bfloat16)

    @pl.when(step == sizes.channels // 2 - 1)
    def _():
        for s in range(samples):
            for cg in range(groups):
                grid_rows = lax.dot_general(
                    x_inverse[...], back[s, cg], (((1,), (1,)), ((), ())),
                    preferred_element_type=jnp.float32,
                )
                rows = pl.ds(cg * sizes.piece, sizes.piece)
                rows_out[:, s, rows] = grid_rows.astype(jnp.bfloat16).reshape(
                    sizes.gx_count, sizes.piece, 128
                )


def inverse_kernel(
    sizes, grid_rows, dz, bypass, y_inverse, time_inverse, spread, input_grad, time_rows, mixer, acc
):
    step = pl.program_id(0)
    channels, group, cells_y = sizes.channels, sizes.group, sizes.cells_y

    @pl.when(step == 0)
    def _():
        joined = jnp.concatenate(
            [
                grid_rows[:, pl.ds(cg * sizes.piece, sizes.piece)].reshape(-1, 128)
                for cg in range(sizes.groups)
            ],
            axis=1,
        )
        total = sizes.devices * sizes.piece
        long = jnp.dot(
            y_inverse[...], spread_rows(sizes, (2 * sizes.modes_y, total), 1),
            preferred_element_type=jnp.float32,
        )
        cell = lax.broadcasted_iota(jnp.int32, long.shape, 1) // 2 % sizes.slab
        for x in range(sizes.slab):
            table = jnp.where(cell == x, long, 0.0).astype(jnp.bfloat16)
            time_rows[pl.ds(x * 2 * cells_y, 2 * cells_y)] = jnp.dot(
                table, joined, preferred_element_type=jnp.float32
            ).astype(jnp.bfloat16)
        tall = jnp.dot(spread[...], bypass[...], preferred_element_type=jnp.float32)
        wide = lax.dot_general(
            tall.astype(jnp.bfloat16), spread[...], (((1,), (1,)), ((), ())),
            preferred_element_type=jnp.float32,
        )
        row = lax.broadcasted_iota(jnp.int32, wide.shape, 0) % 16
        column = lax.broadcasted_iota(jnp.int32, wide.shape, 1) % 16
        mixer[...] = jnp.where(row == column, wide, 0.0).astype(jnp.bfloat16)

    first = pl.multiple_of(step * 2 * cells_y, 2 * cells_y)
    for cg in range(sizes.groups):
        lanes = pl.ds(cg * 128, 128)
        left = jnp.concatenate(
            [time_rows[pl.ds(first + q * cells_y, cells_y), lanes] for q in range(2)], axis=1
        )
        spectral = jnp.dot(left, time_inverse[...], preferred_element_type=jnp.float32)
        for c in range(group):
            acc[cg * group + c] = sizes.scale_in * spectral[:, c * 128 : (c + 1) * 128]
    for block in range(cells_y // 16):
        rows = pl.ds(block * 16, 16)
        mixed = jnp.dot(
            mixer[...], dz[:, 0, rows].reshape(-1, 128), preferred_element_type=jnp.float32
        ).reshape(channels, 16, 128)
        input_grad[0, :, 0, rows] = (mixed + acc[:, rows]).astype(jnp.bfloat16)


def exchange_kernel(gx_count, packet, landed, stage, near, send_sem, recv_sem, own_sem):
    place, core = lax.axis_index("gx"), lax.axis_index("sa")
    sibling = 1 - core
    mesh_ids = dict(device_id_type=pl.DeviceIdType.MESH)
    barrier = pltpu.get_barrier_semaphore()
    pl.semaphore_signal(barrier, inc=1, device_id=(place, sibling), **mesh_ids)

    @pl.loop(1, gx_count)
    def _(step):
        other = (place + step) % gx_count
        pl.semaphore_signal(barrier, inc=1, device_id=(other, core), **mesh_ids)

    pl.semaphore_wait(barrier, gx_count)
    across = pltpu.make_async_remote_copy(
        src_ref=packet.at[:, sibling], dst_ref=stage, send_sem=near.at[0], recv_sem=near.at[1],
        device_id=(place, sibling), **mesh_ids,
    )
    across.start()

    def send(which, step):
        other = (place + step) % gx_count
        source = packet.at[other, core] if which == 0 else stage.at[other]
        return pltpu.make_async_remote_copy(
            src_ref=source,
            dst_ref=landed.at[place, core if which == 0 else sibling],
            send_sem=send_sem.at[which, step],
            recv_sem=recv_sem.at[which, step],
            device_id=(other, core),
            **mesh_ids,
        )

    @pl.loop(1, gx_count)
    def _(step):
        send(0, step).start()

    own = pltpu.make_async_copy(packet.at[place, core], landed.at[place, core], own_sem.at[0])
    own.start()
    across.wait()

    @pl.loop(1, gx_count)
    def _(step):
        send(1, step).start()

    passed = pltpu.make_async_copy(stage.at[place], landed.at[place, sibling], own_sem.at[1])
    passed.start()
    own.wait()
    passed.wait()
    for which in range(2):

        @pl.loop(1, gx_count)
        def _(step):
            send(which, step).wait()


def exchange(packet, sizes, collective_id):
    return pl.pallas_call(
        functools.partial(exchange_kernel, sizes.gx_count),
        in_specs=[pl.BlockSpec(memory_space=pl.ANY)],
        out_specs=pl.BlockSpec(memory_space=pl.ANY),
        out_shape=jax.ShapeDtypeStruct(packet.shape, packet.dtype),
        scratch_shapes=[
            pltpu.VMEM((sizes.gx_count,) + packet.shape[2:], packet.dtype),
            pltpu.SemaphoreType.DMA((2,)),
            pltpu.SemaphoreType.DMA((2, sizes.gx_count)),
            pltpu.SemaphoreType.DMA((2, sizes.gx_count)),
            pltpu.SemaphoreType.DMA((2,)),
        ],
        compiler_params=pltpu.CompilerParams(
            collective_id=collective_id, has_side_effects=True, vmem_limit_bytes=VMEM_BYTES
        ),
        name="exchange",
    )(packet)


def whole(table):
    return pl.BlockSpec(table.shape, lambda *_: (0,) * table.ndim)


def shards(inputs, preact, cotangent, mode_weight, bypass_weight):
    sizes = Sizes(inputs.shape, mode_weight.shape, lax.axis_size("gx"), lax.axis_size("sa"))
    if not sizes.fits():
        return plain_shards(inputs, preact, cotangent, mode_weight, bypass_weight)
    tables_built = [jnp.asarray(table) for table in block_tables(sizes)]
    time_forward, time_inverse, y_forward, y_inverse, x_input, x_grad, x_inverse = tables_built
    channels, slab, cells_y, cells_time = inputs.shape[1:]
    params = pltpu.CompilerParams(vmem_limit_bytes=VMEM_BYTES)
    field_block = pl.BlockSpec(
        (1, channels, 1, cells_y, cells_time), lambda x: (0, 0, x, 0, 0)
    )
    dz_block = pl.BlockSpec((channels, 1, cells_y, cells_time), lambda x: (0, x, 0, 0))
    packet = (sizes.devices, 2 * sizes.groups * sizes.piece, 128)
    rows_shape = (2 * slab * cells_y, sizes.groups * 128)
    dz, spectra = pl.pallas_call(
        functools.partial(forward_kernel, sizes),
        grid=(slab,),
        in_specs=[field_block] * 3 + [whole(time_forward), whole(y_forward)],
        out_specs=[dz_block, pl.BlockSpec(packet, lambda x: (0,) * 3)],
        out_shape=[
            jax.ShapeDtypeStruct(inputs.shape[1:], jnp.bfloat16),
            jax.ShapeDtypeStruct(packet, jnp.bfloat16),
        ],
        scratch_shapes=[pltpu.VMEM(rows_shape, jnp.bfloat16)] * 2
        + [pltpu.VMEM((sizes.devices * sizes.piece, rows_shape[0]), jnp.bfloat16)],
        compiler_params=params,
        name="forward",
    )(inputs, preact, cotangent, time_forward, y_forward)
    spectra = exchange(
        spectra.reshape((sizes.gx_count, sizes.sa_count) + packet[1:]), sizes, 0
    )
    own = sizes.own_pairs
    out_packet = (sizes.gx_count, sizes.sa_count, sizes.groups * sizes.piece, 128)
    mode_grad, grid_rows = pl.pallas_call(
        functools.partial(mode_kernel, sizes),
        grid=(channels // 2,),
        in_specs=[
            whole(spectra),
            pl.BlockSpec(
                (2, channels, own, 128), lambda i: (i, 0, lax.axis_index("sa"), 0)
            ),
            whole(x_input),
            whole(x_grad),
            whole(x_inverse),
        ],
        out_specs=[
            pl.BlockSpec((2, channels, own, 128), lambda i: (i, 0, 0, 0)),
            pl.BlockSpec(out_packet, lambda i: (0,) * 4),
        ],
        out_shape=[
            jax.ShapeDtypeStruct((channels, channels, own, 128), jnp.float32),
            jax.ShapeDtypeStruct(out_packet, jnp.bfloat16),
        ],
        scratch_shapes=[
            pltpu.VMEM((4, sizes.sa_count, channels, own, 128), jnp.float32),
            pltpu.VMEM((sizes.sa_count, sizes.groups, 128, sizes.rows * 128), jnp.bfloat16),
        ],
        compiler_params=params,
        name="modes",
    )(spectra, mode_weight, x_input, x_grad, x_inverse)
    grid_rows = exchange(grid_rows, sizes, 1)
    grid_rows = grid_rows.reshape((sizes.devices,) + out_packet[2:])
    spread = jnp.asarray(np.repeat(np.eye(channels), 16, axis=0).astype(jnp.bfloat16))
    input_grad = pl.pallas_call(
        functools.partial(inverse_kernel, sizes),
        grid=(slab,),
        in_specs=[
            whole(grid_rows), dz_block, whole(bypass_weight), whole(y_inverse),
            whole(time_inverse), whole(spread),
        ],
        out_specs=field_block,
        out_shape=jax.ShapeDtypeStruct(inputs.shape, jnp.bfloat16),
        scratch_shapes=[
            pltpu.VMEM(rows_shape, jnp.bfloat16),
            pltpu.VMEM((channels * 16, channels * 16), jnp.bfloat16),
            pltpu.VMEM((channels, cells_y, cells_time), jnp.float32),
        ],
        compiler_params=params,
        name="inverse",
    )(grid_rows, dz, bypass_weight, y_inverse, time_inverse, spread)
    return input_grad, mode_grad


def solution(mesh):
    placed = (
        P("sa", None, "gx", None, None),
        P("sa", None, "gx", None, None),
        P("sa", None, "gx", None, None),
        P(None, None, "gx", None),
        P(),
    )
    return jax.shard_map(
        shards,
        mesh=mesh,
        in_specs=placed,
        out_specs=(P("sa", None, "gx", None, None), P(None, None, ("gx", "sa"), None)),
        check_vma=False,
    )
```

```python
import functools
import math

import jax
import jax.numpy as jnp
import numpy as np
from jax import lax
from jax.experimental import pallas as pl
from jax.experimental.pallas import tpu as pltpu
from jax.sharding import PartitionSpec as P

MY = 64
MT = 32
VMEM_BYTES = 60 * 2**20


root_half = math.sqrt(0.5)
gauss_norm = 1.0 / math.sqrt(2.0 * math.pi)


def tables(kept_count, length, two_sided):
    frequency = jnp.arange(kept_count, dtype=jnp.int32)
    if two_sided:
        frequency = jnp.where(
            frequency < kept_count // 2, frequency, frequency + (length - kept_count)
        )
    position = jnp.arange(length, dtype=jnp.int32)
    product = frequency[:, None] * position[None, :] % length
    phase_angle = product.astype(jnp.float32) * (2.0 * math.pi / length)
    return (jnp.cos(phase_angle).astype(jnp.bfloat16), jnp.sin(phase_angle).astype(jnp.bfloat16))


def gelu_backward(preact_block, cotangent_block):
    values = preact_block.astype(jnp.float32)
    slope = (
        0.5 * (1.0 + jax.scipy.special.erf(values * root_half))
        + values * jnp.exp(-0.5 * values * values) * gauss_norm
    )
    return (cotangent_block.astype(jnp.float32) * slope).astype(jnp.bfloat16)


def gradient_term(input_hat, grad_hat, half):
    input_real = input_hat[..., :half].astype(jnp.float32)[:, None]
    input_imag = input_hat[..., half:].astype(jnp.float32)[:, None]
    grad_real = grad_hat[..., :half].astype(jnp.float32)[None]
    grad_imag = grad_hat[..., half:].astype(jnp.float32)[None]
    return jnp.concatenate(
        [
            input_real * grad_real + input_imag * grad_imag,
            input_real * grad_imag - input_imag * grad_real,
        ],
        axis=-1,
    )


def plain_shards(inputs, preact, cotangent, mode_weight, bypass_weight):
    channels = inputs.shape[1]
    slab_cells = inputs.shape[2]
    cells_y = inputs.shape[3]
    cells_time = inputs.shape[4]
    devices_x = lax.axis_size("gx")
    cells_x = slab_cells * devices_x
    modes_x = mode_weight.shape[3] // 2
    modes_y = MY
    modes_time = MT
    pair_count = modes_y * modes_time
    cell_count = cells_x * cells_y * cells_time
    scale_in = float(modes_x * pair_count * cell_count) ** (-0.25)
    scale_out = float(cell_count) ** (-0.5)
    cosine_time, sine_time = tables(modes_time, cells_time, False)
    cosine_y, sine_y = tables(modes_y, cells_y, True)
    cosine_x, sine_x = tables(modes_x, cells_x, True)
    forward_time = jnp.concatenate([cosine_time.T, -sine_time.T], axis=1)
    inverse_time = jnp.concatenate([cosine_time, -sine_time], axis=0)
    plane_table = jnp.stack([jnp.stack([cosine_y, sine_y], -1), jnp.stack([-sine_y, cosine_y], -1)])
    x_forward = jnp.stack(
        [jnp.concatenate([cosine_x, -sine_x], 0).T, jnp.concatenate([sine_x, cosine_x], 0).T], 1
    )
    x_inverse = jnp.stack(
        [jnp.concatenate([cosine_x, -sine_x], 0), jnp.concatenate([sine_x, cosine_x], 0)], -1
    )

    def spectra(field):
        sectioned = jnp.dot(
            field.reshape(-1, cells_time), forward_time, preferred_element_type=jnp.float32
        ).astype(jnp.bfloat16)
        sectioned = sectioned.reshape(channels, slab_cells, cells_y, 2, modes_time)
        plane = jnp.einsum(
            "cxyqk,ajyq->jkcxa", sectioned, plane_table, preferred_element_type=jnp.float32
        ).astype(jnp.bfloat16)
        return plane.reshape(pair_count, channels, slab_cells, 2)

    def x_transform(block, factor):
        summed = jnp.einsum("pcxq,xqr->cpr", block, x_forward, preferred_element_type=jnp.float32)
        return (factor * summed).astype(jnp.bfloat16)

    dz_field = gelu_backward(preact[0], cotangent[0])
    input_hat = x_transform(
        lax.all_to_all(spectra(inputs[0]), "gx", split_axis=0, concat_axis=2, tiled=True), scale_in
    )
    grad_hat = x_transform(
        lax.all_to_all(spectra(dz_field), "gx", split_axis=0, concat_axis=2, tiled=True), scale_out
    )
    mode_grad = lax.psum_scatter(
        gradient_term(input_hat, grad_hat, modes_x).astype(jnp.bfloat16),
        "sa",
        scatter_dimension=2,
        tiled=True,
    ).astype(jnp.float32)
    weights = mode_weight.astype(jnp.float32)
    grad_real = grad_hat[..., :modes_x].astype(jnp.float32)[None]
    grad_imag = grad_hat[..., modes_x:].astype(jnp.float32)[None]
    weight_real = weights[..., :modes_x]
    weight_imag = weights[..., modes_x:]
    back_real = jnp.sum(weight_real * grad_real + weight_imag * grad_imag, axis=1)
    back_imag = jnp.sum(weight_real * grad_imag - weight_imag * grad_real, axis=1)
    back_hat = jnp.concatenate([back_real, back_imag], axis=-1).astype(jnp.bfloat16)
    grid_rows = jnp.einsum(
        "cpr,rxq->pcxq", back_hat, x_inverse, preferred_element_type=jnp.float32
    ).astype(jnp.bfloat16)
    block = lax.all_to_all(grid_rows, "gx", split_axis=2, concat_axis=0, tiled=True)
    items = block.shape[1]
    plane = block.reshape(modes_y, modes_time, items, slab_cells, 2)
    joined = jnp.einsum(
        "jkcxa,ajyq->cxyqk", plane, plane_table, preferred_element_type=jnp.float32
    ).astype(jnp.bfloat16)
    spectral = jnp.dot(
        joined.reshape(-1, 2 * modes_time), inverse_time, preferred_element_type=jnp.float32
    )
    spectral_grad = scale_in * spectral.reshape(items, slab_cells, cells_y, cells_time)
    bypass = jnp.dot(
        bypass_weight, dz_field.reshape(channels, -1), preferred_element_type=jnp.float32
    ).reshape(dz_field.shape)
    input_grad = (spectral_grad + bypass).astype(jnp.bfloat16)[None]
    return (input_grad, mode_grad)


def host_tables(kept_count, length, two_sided):
    frequency = np.arange(kept_count)
    if two_sided:
        frequency = np.where(
            frequency < kept_count // 2, frequency, frequency + (length - kept_count)
        )
    product = frequency[:, None] * np.arange(length)[None, :] % length
    angle = product.astype(np.float32) * np.float32(2.0 * math.pi / length)
    return np.cos(angle).astype(np.float32), np.sin(angle).astype(np.float32)


def block_tables(sizes):
    ct, st = host_tables(sizes.modes_time, sizes.cells_time, False)
    cy, sy = host_tables(sizes.modes_y, sizes.cells_y, True)
    cx, sx = host_tables(sizes.modes_x, sizes.cells_x, True)
    group = np.eye(sizes.group, dtype=np.float32)
    rows = np.eye(sizes.rows, dtype=np.float32)
    time = np.stack([ct, -st])
    time_forward = np.einsum("cd,qkt->ctqdk", group, time)
    time_forward = time_forward.reshape(sizes.group * sizes.cells_time, -1)
    time_inverse = time_forward.T
    plane = np.stack([np.stack([cy, sy]), np.stack([-sy, cy])])
    plane = plane.reshape(2, 2, sizes.devices, sizes.rows, sizes.cells_y)
    plane = np.einsum("qpdjy->djqpy", plane)
    y_forward = plane.reshape(2 * sizes.modes_y, -1)
    y_inverse = y_forward.T
    x_table = np.stack(
        [np.concatenate([cx, -sx], 0).T, np.concatenate([sx, cx], 0).T], 1
    )
    x_table = x_table.reshape(-1, sizes.slab, 2, 2 * sizes.modes_x)
    real, imag = x_table[..., : sizes.modes_x], x_table[..., sizes.modes_x :]

    def x_rows(table):
        wide = np.einsum("gxqr,jl->gjxqlr", table, rows)
        return wide.reshape(-1, sizes.rows * table.shape[-1])

    x_input = x_rows(np.concatenate([real, real, imag, imag], -1))
    x_grad = x_rows(np.concatenate([real, imag, imag, -real], -1))
    x_inverse = x_rows(x_table)
    everything = (time_forward, time_inverse, y_forward, y_inverse, x_input, x_grad, x_inverse)
    return [table.astype(jnp.bfloat16) for table in everything]


class Sizes:
    def __init__(self, inputs, mode_weight, gx_count, sa_count):
        _, self.channels, self.slab, self.cells_y, self.cells_time = inputs
        self.modes_x = mode_weight[3] // 2
        self.modes_y, self.modes_time = MY, MT
        self.gx_count, self.sa_count = gx_count, sa_count
        self.devices = gx_count * sa_count
        self.cells_x = self.slab * gx_count
        self.pairs = self.modes_y * self.modes_time
        self.own_pairs = self.pairs // self.devices
        self.rows = self.own_pairs // self.modes_time
        self.piece = self.rows * self.slab * 2
        self.group = 128 // self.modes_time
        self.groups = self.channels // self.group
        cell_count = self.cells_x * self.cells_y * self.cells_time
        self.scale_in = float(self.modes_x * self.pairs * cell_count) ** (-0.25)
        self.scale_out = float(cell_count) ** (-0.5)

    def fits(self):
        return (
            self.own_pairs == self.rows * self.modes_time
            and self.own_pairs % 16 == 0
            and self.piece % 16 == 0
            and self.modes_x == 64
            and self.channels % self.group == 0
            and self.cells_time == 128
            and self.cells_y == 128
            and inputs_fit(self)
        )


def inputs_fit(sizes):
    return sizes.sa_count == 2 and sizes.channels == 16


def spread_rows(sizes, shape, dim):
    tall = lax.broadcasted_iota(jnp.int32, shape, dim)
    short = lax.broadcasted_iota(jnp.int32, shape, 1 - dim)
    meets = tall // (2 * sizes.slab) * 2 + tall % 2 == short
    return jnp.where(meets, 1.0, 0.0).astype(jnp.bfloat16)


def forward_kernel(
    sizes, inputs, preact, cotangent, time_forward, y_forward, dz, spectra, in_rows, dz_rows, wide
):
    step = pl.program_id(0)
    slope = gelu_slope(preact[0, :, 0].astype(jnp.float32))
    gradient = (cotangent[0, :, 0].astype(jnp.float32) * slope).astype(jnp.bfloat16)
    dz[:, 0] = gradient
    first = pl.multiple_of(step * 2 * sizes.cells_y, 2 * sizes.cells_y)

    def time_rows(read, target):
        for cg in range(sizes.groups):
            left = jnp.concatenate(
                [read(cg * sizes.group + c) for c in range(sizes.group)], axis=1
            )
            both = jnp.dot(left, time_forward[...], preferred_element_type=jnp.float32)
            both = both.astype(jnp.bfloat16)
            for q in range(2):
                target[pl.ds(first + q * sizes.cells_y, sizes.cells_y), pl.ds(cg * 128, 128)] = (
                    both[:, q * 128 : (q + 1) * 128]
                )

    time_rows(lambda c: inputs[0, c, 0], in_rows)
    time_rows(lambda c: dz[c, 0], dz_rows)

    @pl.when(step == 0)
    def _():
        total = sizes.devices * sizes.piece
        tall = jnp.dot(
            spread_rows(sizes, (total, 2 * sizes.modes_y), 0), y_forward[...],
            preferred_element_type=jnp.float32,
        )
        cell = lax.broadcasted_iota(jnp.int32, tall.shape, 0) // 2 % sizes.slab
        for x in range(sizes.slab):
            wide[:, pl.ds(x * tall.shape[1], tall.shape[1])] = jnp.where(
                cell == x, tall, 0.0
            ).astype(jnp.bfloat16)

    @pl.when(step == sizes.slab - 1)
    def _():
        for field, held in enumerate((in_rows, dz_rows)):
            plane = jnp.dot(wide[...], held[...], preferred_element_type=jnp.float32)
            plane = plane.astype(jnp.bfloat16)
            for cg in range(sizes.groups):
                rows = pl.ds((field * sizes.groups + cg) * sizes.piece, sizes.piece)
                spectra[:, rows] = plane[:, cg * 128 : (cg + 1) * 128].reshape(
                    sizes.devices, sizes.piece, 128
                )


def gelu_slope(values):
    return (
        0.5 * (1.0 + lax.erf(values * root_half))
        + values * jnp.exp(-0.5 * values * values) * gauss_norm
    )


def mode_kernel(
    sizes, spectra, weight, x_input, x_grad, x_inverse, mode_grad, rows_out, hats, back
):
    step = pl.program_id(0)
    samples, groups, kt = sizes.sa_count, sizes.groups, sizes.modes_time

    @pl.when(step == 0)
    def _():
        for field, table, scale in (
            (0, x_input, sizes.scale_in),
            (1, x_grad, sizes.scale_out),
        ):
            for s in range(samples):
                for cg in range(groups):
                    first = (field * groups + cg) * sizes.piece
                    block = spectra[:, s, pl.ds(first, sizes.piece)].reshape(-1, 128)
                    summed = lax.dot_general(
                        block, table[...], (((0,), (0,)), ((), ())),
                        preferred_element_type=jnp.float32,
                    )
                    summed = (scale * summed).astype(jnp.bfloat16).astype(jnp.float32)
                    for j in range(sizes.rows):
                        for part in range(2):
                            lanes = (2 * j + part) * 128
                            for c in range(sizes.group):
                                hats[
                                    2 * field + part, s, cg * sizes.group + c, pl.ds(j * kt, kt)
                                ] = summed[c * kt : (c + 1) * kt, lanes : lanes + 128]

    low = lax.broadcasted_iota(jnp.int32, (16, 128), 1) < sizes.modes_x
    for index in range(4 * (sizes.own_pairs // 16)):
        within, block = index // (sizes.own_pairs // 16), index % (sizes.own_pairs // 16)
        channel = step * 4 + within
        cg, member = channel // sizes.group, channel % sizes.group
        rows = pl.ds(block * 16, 16)
        left = [[hats[part, s, channel, rows] for s in range(samples)] for part in range(2)]
        total = [[None, None] for _ in range(samples)]
        for o in range(sizes.channels):
            right = [[hats[2 + part, s, o, rows] for s in range(samples)] for part in range(2)]
            value = weight[within, o, rows].astype(jnp.float32)
            grad = None
            for s in range(samples):
                for part in range(2):
                    term = left[part][s] * right[part][s]
                    grad = term if grad is None else grad + term
                    term = value * right[part][s]
                    held = total[s][part]
                    total[s][part] = term if held is None else held + term
            mode_grad[within, o, rows] = grad
        j, k = divmod(block * 16, kt)
        for s in range(samples):
            real, imag = total[s]
            real = real + pltpu.roll(real, sizes.modes_x, 1)
            imag = imag + pltpu.roll(imag, sizes.modes_x, 1)
            first = pl.multiple_of(member * kt + k, 16)
            back[s, cg, pl.ds(first, 16), pl.ds(j * 128, 128)] = jnp.where(
                low, real, imag
            ).astype(jnp.bfloat16)

    @pl.when(step == sizes.channels // 4 - 1)
    def _():
        for s in range(samples):
            for cg in range(groups):
                grid_rows = lax.dot_general(
                    x_inverse[...], back[s, cg], (((1,), (1,)), ((), ())),
                    preferred_element_type=jnp.float32,
                )
                rows = pl.ds(cg * sizes.piece, sizes.piece)
                rows_out[:, s, rows] = grid_rows.astype(jnp.bfloat16).reshape(
                    sizes.gx_count, sizes.piece, 128
                )


def inverse_kernel(
    sizes, grid_rows, dz, bypass, y_inverse, time_inverse, spread, input_grad, time_rows, mixer, acc
):
    step = pl.program_id(0)
    channels, group, cells_y = sizes.channels, sizes.group, sizes.cells_y

    @pl.when(step == 0)
    def _():
        joined = jnp.concatenate(
            [
                grid_rows[:, pl.ds(cg * sizes.piece, sizes.piece)].reshape(-1, 128)
                for cg in range(sizes.groups)
            ],
            axis=1,
        )
        total = sizes.devices * sizes.piece
        long = jnp.dot(
            y_inverse[...], spread_rows(sizes, (2 * sizes.modes_y, total), 1),
            preferred_element_type=jnp.float32,
        )
        cell = lax.broadcasted_iota(jnp.int32, long.shape, 1) // 2 % sizes.slab
        for x in range(sizes.slab):
            table = jnp.where(cell == x, long, 0.0).astype(jnp.bfloat16)
            time_rows[pl.ds(x * 2 * cells_y, 2 * cells_y)] = jnp.dot(
                table, joined, preferred_element_type=jnp.float32
            ).astype(jnp.bfloat16)
        tall = jnp.dot(spread[...], bypass[...], preferred_element_type=jnp.float32)
        wide = lax.dot_general(
            tall.astype(jnp.bfloat16), spread[...], (((1,), (1,)), ((), ())),
            preferred_element_type=jnp.float32,
        )
        row = lax.broadcasted_iota(jnp.int32, wide.shape, 0) % 16
        column = lax.broadcasted_iota(jnp.int32, wide.shape, 1) % 16
        mixer[...] = jnp.where(row == column, wide, 0.0).astype(jnp.bfloat16)

    first = pl.multiple_of(step * 2 * cells_y, 2 * cells_y)
    for cg in range(sizes.groups):
        lanes = pl.ds(cg * 128, 128)
        left = jnp.concatenate(
            [time_rows[pl.ds(first + q * cells_y, cells_y), lanes] for q in range(2)], axis=1
        )
        spectral = jnp.dot(left, time_inverse[...], preferred_element_type=jnp.float32)
        for c in range(group):
            acc[cg * group + c] = sizes.scale_in * spectral[:, c * 128 : (c + 1) * 128]
    for block in range(cells_y // 16):
        rows = pl.ds(block * 16, 16)
        mixed = jnp.dot(
            mixer[...], dz[:, 0, rows].reshape(-1, 128), preferred_element_type=jnp.float32
        ).reshape(channels, 16, 128)
        input_grad[0, :, 0, rows] = (mixed + acc[:, rows]).astype(jnp.bfloat16)


def exchange_kernel(gx_count, packet, landed, stage, near, send_sem, recv_sem, own_sem):
    place, core = lax.axis_index("gx"), lax.axis_index("sa")
    sibling = 1 - core
    mesh_ids = dict(device_id_type=pl.DeviceIdType.MESH)
    barrier = pltpu.get_barrier_semaphore()
    pl.semaphore_signal(barrier, inc=1, device_id=(place, sibling), **mesh_ids)

    @pl.loop(1, gx_count)
    def _(step):
        other = (place + step) % gx_count
        pl.semaphore_signal(barrier, inc=1, device_id=(other, core), **mesh_ids)

    pl.semaphore_wait(barrier, gx_count)
    across = pltpu.make_async_remote_copy(
        src_ref=packet.at[:, sibling], dst_ref=stage, send_sem=near.at[0], recv_sem=near.at[1],
        device_id=(place, sibling), **mesh_ids,
    )
    across.start()

    def send(which, step):
        other = (place + step) % gx_count
        source = packet.at[other, core] if which == 0 else stage.at[other]
        return pltpu.make_async_remote_copy(
            src_ref=source,
            dst_ref=landed.at[place, core if which == 0 else sibling],
            send_sem=send_sem.at[which, step],
            recv_sem=recv_sem.at[which, step],
            device_id=(other, core),
            **mesh_ids,
        )

    @pl.loop(1, gx_count)
    def _(step):
        send(0, step).start()

    own = pltpu.make_async_copy(packet.at[place, core], landed.at[place, core], own_sem.at[0])
    own.start()
    across.wait()

    @pl.loop(1, gx_count)
    def _(step):
        send(1, step).start()

    passed = pltpu.make_async_copy(stage.at[place], landed.at[place, sibling], own_sem.at[1])
    passed.start()
    own.wait()
    passed.wait()
    for which in range(2):

        @pl.loop(1, gx_count)
        def _(step):
            send(which, step).wait()


def exchange(packet, sizes, collective_id):
    return pl.pallas_call(
        functools.partial(exchange_kernel, sizes.gx_count),
        in_specs=[pl.BlockSpec(memory_space=pltpu.VMEM)],
        out_specs=pl.BlockSpec(memory_space=pltpu.VMEM),
        out_shape=jax.ShapeDtypeStruct(packet.shape, packet.dtype),
        scratch_shapes=[
            pltpu.VMEM((sizes.gx_count,) + packet.shape[2:], packet.dtype),
            pltpu.SemaphoreType.DMA((2,)),
            pltpu.SemaphoreType.DMA((2, sizes.gx_count)),
            pltpu.SemaphoreType.DMA((2, sizes.gx_count)),
            pltpu.SemaphoreType.DMA((2,)),
        ],
        compiler_params=pltpu.CompilerParams(
            collective_id=collective_id, has_side_effects=True, vmem_limit_bytes=VMEM_BYTES
        ),
        name="exchange",
    )(packet)


def whole(table):
    return pl.BlockSpec(table.shape, lambda *_: (0,) * table.ndim)


def shards(inputs, preact, cotangent, mode_weight, bypass_weight):
    sizes = Sizes(inputs.shape, mode_weight.shape, lax.axis_size("gx"), lax.axis_size("sa"))
    if not sizes.fits():
        return plain_shards(inputs, preact, cotangent, mode_weight, bypass_weight)
    tables_built = [jnp.asarray(table) for table in block_tables(sizes)]
    time_forward, time_inverse, y_forward, y_inverse, x_input, x_grad, x_inverse = tables_built
    channels, slab, cells_y, cells_time = inputs.shape[1:]
    params = pltpu.CompilerParams(vmem_limit_bytes=VMEM_BYTES)
    field_block = pl.BlockSpec(
        (1, channels, 1, cells_y, cells_time), lambda x: (0, 0, x, 0, 0)
    )
    dz_block = pl.BlockSpec((channels, 1, cells_y, cells_time), lambda x: (0, x, 0, 0))
    packet = (sizes.devices, 2 * sizes.groups * sizes.piece, 128)
    rows_shape = (2 * slab * cells_y, sizes.groups * 128)
    dz, spectra = pl.pallas_call(
        functools.partial(forward_kernel, sizes),
        grid=(slab,),
        in_specs=[field_block] * 3 + [whole(time_forward), whole(y_forward)],
        out_specs=[dz_block, pl.BlockSpec(packet, lambda x: (0,) * 3)],
        out_shape=[
            jax.ShapeDtypeStruct(inputs.shape[1:], jnp.bfloat16),
            jax.ShapeDtypeStruct(packet, jnp.bfloat16),
        ],
        scratch_shapes=[pltpu.VMEM(rows_shape, jnp.bfloat16)] * 2
        + [pltpu.VMEM((sizes.devices * sizes.piece, rows_shape[0]), jnp.bfloat16)],
        compiler_params=params,
        name="forward",
    )(inputs, preact, cotangent, time_forward, y_forward)
    spectra = exchange(
        spectra.reshape((sizes.gx_count, sizes.sa_count) + packet[1:]), sizes, 0
    )
    own = sizes.own_pairs
    out_packet = (sizes.gx_count, sizes.sa_count, sizes.groups * sizes.piece, 128)
    mode_grad, grid_rows = pl.pallas_call(
        functools.partial(mode_kernel, sizes),
        grid=(channels // 4,),
        in_specs=[
            whole(spectra),
            pl.BlockSpec(
                (4, channels, own, 128), lambda i: (i, 0, lax.axis_index("sa"), 0)
            ),
            whole(x_input),
            whole(x_grad),
            whole(x_inverse),
        ],
        out_specs=[
            pl.BlockSpec((4, channels, own, 128), lambda i: (i, 0, 0, 0)),
            pl.BlockSpec(out_packet, lambda i: (0,) * 4),
        ],
        out_shape=[
            jax.ShapeDtypeStruct((channels, channels, own, 128), jnp.float32),
            jax.ShapeDtypeStruct(out_packet, jnp.bfloat16),
        ],
        scratch_shapes=[
            pltpu.VMEM((4, sizes.sa_count, channels, own, 128), jnp.float32),
            pltpu.VMEM((sizes.sa_count, sizes.groups, 128, sizes.rows * 128), jnp.bfloat16),
        ],
        compiler_params=params,
        name="modes",
    )(spectra, mode_weight, x_input, x_grad, x_inverse)
    grid_rows = exchange(grid_rows, sizes, 1)
    grid_rows = grid_rows.reshape((sizes.devices,) + out_packet[2:])
    spread = jnp.asarray(np.repeat(np.eye(channels), 16, axis=0).astype(jnp.bfloat16))
    input_grad = pl.pallas_call(
        functools.partial(inverse_kernel, sizes),
        grid=(slab,),
        in_specs=[
            whole(grid_rows), dz_block, whole(bypass_weight), whole(y_inverse),
            whole(time_inverse), whole(spread),
        ],
        out_specs=field_block,
        out_shape=jax.ShapeDtypeStruct(inputs.shape, jnp.bfloat16),
        scratch_shapes=[
            pltpu.VMEM(rows_shape, jnp.bfloat16),
            pltpu.VMEM((channels * 16, channels * 16), jnp.bfloat16),
            pltpu.VMEM((channels, cells_y, cells_time), jnp.float32),
        ],
        compiler_params=params,
        name="inverse",
    )(grid_rows, dz, bypass_weight, y_inverse, time_inverse, spread)
    return input_grad, mode_grad


def solution(mesh):
    placed = (
        P("sa", None, "gx", None, None),
        P("sa", None, "gx", None, None),
        P("sa", None, "gx", None, None),
        P(None, None, "gx", None),
        P(),
    )
    return jax.shard_map(
        shards,
        mesh=mesh,
        in_specs=placed,
        out_specs=(P("sa", None, "gx", None, None), P(None, None, ("gx", "sa"), None)),
        check_vma=False,
    )
```
